512 devices in a mesh: tile: 128 (over x, y_lo, z), kern: 4 (over y_hi, core).
Axes of the slice: x: 4, y: 4 (y_hi: 2, y_lo: 2; y = y_hi * 2 + y_lo), z: 16, core: 2. Of those that a mesh axis runs over, the one named last changes fastest.
Arguments:
- mask_logit: float32 [16384, 256], P('tile'), may hold values from -6 to 6
- target: int32 [16384, 256], P('tile'), may hold values 0 or 1
- kern_real: float32 [12, 65, 65], P('kern'), may hold values from -0.09375 to 0.09375
- kern_imag: float32 [12, 65, 65], P('kern'), may hold values from -0.09375 to 0.09375
- kern_weight: float32 [12], P('kern'), may hold values from 0.07 to 0.14
Outputs:
- logit_grad: float32 [16384, 256], P('tile', 'kern')
The draws below stay inside these ranges and needn't reach their ends.
All inputs are finite; a program needn't handle non-finite values. No bound on the sum of `target` on one device may be relied on, other than what follows from the above.
Results may differ from the reference program's by a relative error of at most 0.00021.
Values sent between devices are 32-bit elements; how exact they have to be, the bound alone decides.
A program may use at most 64 MiB of HBM per device.

```python
import jax
import jax.numpy as jnp

COLS = 256
TAPS = 65
KERNELS = 12
ROWS = 16384


def place_ends(array, rng, smallest, high):
    dims = array.shape
    index_at = [jax.random.randint(jax.random.fold_in(rng, axis), (), 0, dims[axis]) for axis in range(len(dims))]
    array = array.at[tuple(index_at)].set(smallest)
    longest = dims.index(max(dims))
    index_at[longest] = (index_at[longest] + 1) % dims[longest]
    return array.at[tuple(index_at)].set(high)


def levels(rng, extent, cuts, least, top_value):
    level, own = 1.0, jax.random.fold_in(rng, 6)
    for dim, parts in cuts:
        steps = jnp.exp(jax.random.uniform(jax.random.fold_in(own, dim), (parts,), jnp.float32, least / len(cuts), top_value / len(cuts)))
        level = level * jnp.repeat(steps, extent[dim] // parts).reshape([-1 if axis == dim else 1 for axis in range(len(extent))])
    return level


def gaussian(key, dims, scale, reach, cuts=(), dtype=jnp.bfloat16):
    values = scale * jax.random.normal(key, dims, jnp.float32)
    if cuts:
        values = values * levels(key, dims, cuts, -0.22, 0.18)
    return jnp.clip(values, -reach, reach).astype(dtype)


def setup_inputs(seed: int = 0) -> dict:
    keys = jax.random.split(jax.random.key(seed), 6)
    return {
        "mask_logit": gaussian(keys[0], (ROWS, COLS), 1.0, 6.0, ((0, 128),), jnp.float32),
        "target": place_ends((jax.random.randint(keys[1], (ROWS, COLS), 0, 2) < 1).astype(jnp.int32), jax.random.fold_in(keys[1], 1), 0, 1),
        "kern_real": gaussian(keys[2], (KERNELS, TAPS, TAPS), (TAPS * TAPS) ** -0.5, 0.09375, ((0, 4),), jnp.float32),
        "kern_imag": gaussian(keys[3], (KERNELS, TAPS, TAPS), (TAPS * TAPS) ** -0.5, 0.09375, ((0, 4),), jnp.float32),
        "kern_weight": jnp.clip(0.07 + 0.07 * jax.random.uniform(keys[4], (KERNELS,), jnp.float32) ** levels(keys[4], (KERNELS,), ((0, 4),), -0.2, 0.2), 0.07, 0.14),
    }


MASK_SLOPE = 3.0
RESIST_SLOPE = 6.0
RESIST_LEVEL = 1.0

def place_taps(taps_grid, row_len, col_len, radius):
    tap_count = taps_grid.shape[0]
    flipped = taps_grid[::-1, ::-1]
    spread = jnp.pad(flipped, ((0, row_len - tap_count), (0, col_len - tap_count)))
    return jnp.roll(spread, (-radius, -radius), (0, 1))

def reference(mask_logit, target, kern_real, kern_imag, kern_weight):
    radius = (TAPS - 1) // 2
    row_total, col_total = mask_logit.shape
    target_value = target.astype(jnp.float32)

    def loss_of(logits):
        mask_value = jax.nn.sigmoid(MASK_SLOPE * logits)
        padded = jnp.pad(mask_value, radius)
        row_len, col_len = padded.shape
        spectrum = jnp.fft.fft2(padded)
        intensity = jnp.zeros_like(mask_value)
        for kernel_index in range(KERNELS):
            spread_real = place_taps(kern_real[kernel_index], row_len, col_len, radius)
            spread_imag = place_taps(kern_imag[kernel_index], row_len, col_len, radius)
            kernel_spec = jnp.fft.fft2(spread_real) + 1j * jnp.fft.fft2(spread_imag)
            light_field = jnp.fft.ifft2(spectrum * kernel_spec)[radius:radius + row_total, radius:radius + col_total]
            intensity = intensity + kern_weight[kernel_index] * (jnp.real(light_field) ** 2 + jnp.imag(light_field) ** 2)
        printed = jax.nn.sigmoid(RESIST_SLOPE * (intensity - RESIST_LEVEL))
        return jnp.sum((printed - target_value) ** 2)
    return jax.grad(loss_of)(mask_logit)
```

```python
import functools
import math

import jax
import jax.numpy as jnp
import ml_dtypes
import numpy as np
from jax import lax
from jax.experimental import pallas as pl
from jax.experimental.pallas import tpu as pltpu
from jax.sharding import PartitionSpec as P

F32 = jnp.float32
BF16 = jnp.bfloat16
MESH = pl.DeviceIdType.MESH

BAND = 128
COLS = 256
TAPS = 65
RADIUS = 32
OWN = 3
BOTH = 2 * OWN
NX = 224
FX = NX // 2
NY = 256
FIELD = 160
FROWS = 192


def pair(table):
    high = table.astype(ml_dtypes.bfloat16)
    low = (table - high.astype(np.float64)).astype(ml_dtypes.bfloat16)
    return np.stack([high, low])


def tables():
    theta = 2.0 * np.pi * (np.arange(FX) + 0.5) / NX

    def wave(offsets):
        angle = theta[:, None] * offsets[None, :]
        return np.concatenate([np.cos(angle), -np.sin(angle)], 0)

    scale = 2.0 / (NX * NY)
    into, back_in, out, last, pick = [], [], [], [], []
    for half in range(2):
        local = np.arange(COLS) - 64 * half
        full = wave(local) * ((local >= 0) & (local < 192))[None, :]
        into.append(pair(full))
        part = full[:, 96 * half : 96 * half + FIELD]
        back_in.append(pair(part))
        out.append(pair(scale * part.T))
        for core in range(2):
            cols = np.concatenate([64 * (2 * half + c) + np.arange(64) for c in (core, 1 - core)])
            last.append(pair(2.0 * scale * full[:, cols].T))
        pick.append((np.arange(COLS)[None, :] == np.arange(FIELD)[:, None] + 96 * half))
    taps = wave(np.arange(64) - RADIUS)
    zero = np.zeros_like(taps)
    taps = np.concatenate([np.concatenate([taps, zero], 1), np.concatenate([zero, taps], 1)], 0)
    edge = np.broadcast_to(wave(np.array([RADIUS])), (NX, 128))
    rows = []
    for odd in range(2):
        angle = 2.0 * np.pi * np.arange(128)[:, None] * (2 * np.arange(128) + odd)[None, :] / NY
        c, s = np.cos(angle), np.sin(angle)
        rows.append(pair(np.concatenate([np.concatenate([c, -s], 1), np.concatenate([s, c], 1)], 0)))
    return dict(
        rows=np.stack(rows),
        into=np.stack(into),
        taps=pair(taps),
        edge=edge.astype(np.float32),
        out=np.stack(out),
        back_in=np.stack(back_in),
        last=np.stack(last),
        pick=np.stack(pick).astype(ml_dtypes.bfloat16),
    )


NAMES = ("taps", "edge", "rows", "into", "out", "pick", "back_in", "last")


def split(value):
    high = value.astype(BF16)
    return high, (value - high.astype(F32)).astype(BF16)


def dot(left, right):
    return jnp.dot(left, right, preferred_element_type=F32)


def dot_t(left, right):
    return lax.dot_general(left, right, (((1,), (1,)), ((), ())), preferred_element_type=F32)


def right_mul(value, table, mul):
    high, low = split(value)
    count = value.shape[0]
    both = mul(jnp.concatenate([high, low], 0), table[0])
    return both[:count] + both[count:] + mul(high, table[1])


def left_mul(table, value, mul):
    high, low = split(value)
    return mul(table[0], high) + mul(table[1], high) + mul(table[0], low)


def kernel(
    logit, target, kern_real, kern_imag, weight, taps_h, edge_h, rows_h, into_h, out_h, pick_h, back_h, last_h,
    result,
    ext, goal, kr, ki, w, taps_c, edge_c, rows_c, into_c, out_c, pick_c, back_c, last_c,
    packed, spec, fields, part, part_in, grad, grad_in,
    local_sem, send_sem, recv_sem,
):
    tile, kern = lax.axis_index("tile"), lax.axis_index("kern")
    tiles = lax.axis_size("tile")
    half, core = kern // 2, lax.rem(kern, 2)
    before = {"tile": lax.rem(tile + tiles - 1, tiles)}
    after = {"tile": lax.rem(tile + 1, tiles)}
    mate = {"kern": 2 * half + (1 - core)}
    across = {"kern": 2 * (1 - half) + core}

    barrier = pltpu.get_barrier_semaphore()
    for device in (before, after, across, mate):
        pl.semaphore_signal(barrier, inc=1, device_id=device, device_id_type=MESH)

    pairs = (
        (kern_real, kr),
        (kern_imag, ki),
        (weight, w),
        (taps_h, taps_c),
        (edge_h, edge_c),
        (rows_h, rows_c),
        (logit, ext.at[pl.ds(64, BAND)]),
        (into_h.at[half], into_c),
        (out_h.at[half], out_c),
        (target, goal.at[pl.ds(RADIUS, BAND)]),
        (pick_h.at[half], pick_c),
        (back_h.at[half], back_c),
        (last_h.at[kern], last_c),
    )
    loads = [pltpu.make_async_copy(src, dst, local_sem.at[i]) for i, (src, dst) in enumerate(pairs)]
    for load in loads:
        load.start()

    def send(index, src, dst, device):
        copy = pltpu.make_async_remote_copy(
            src_ref=src, dst_ref=dst, send_sem=send_sem.at[index], recv_sem=recv_sem.at[index],
            device_id=device, device_id_type=MESH,
        )
        copy.start()
        return copy

    for load in loads[:3]:
        load.wait()
    eye = lax.broadcasted_iota(jnp.int32, (TAPS, 128), 0) == lax.broadcasted_iota(jnp.int32, (TAPS, 128), 1)
    ends = []
    for k in range(OWN):
        factor = jnp.sqrt(jnp.full((TAPS, TAPS), w[k], F32))
        real, imag = kr[k] * factor, ki[k] * factor
        packed[k, 0:72, :] = jnp.zeros((72, 128), F32)
        packed[k, 0:TAPS, :] = jnp.concatenate([real[:, 0:64], imag[:, 0:64]], axis=1)
        for grid in (real, imag):
            column = jnp.broadcast_to(grid[:, 64:65], (TAPS, 128))
            ends.append(jnp.sum(jnp.where(eye, column, 0.0), axis=0, keepdims=True))
    row_id = lax.broadcasted_iota(jnp.int32, (8, 128), 0)
    end_rows = jnp.zeros((8, 128), F32)
    for i, end in enumerate(ends):
        end_rows = jnp.where(row_id == i, jnp.broadcast_to(end, (8, 128)), end_rows)
    packed[OWN, 0:72, :] = jnp.zeros((72, 128), F32)
    packed[OWN, 0:8, :] = end_rows

    pl.semaphore_wait(barrier, 4)
    sends = [
        send(0, packed.at[pl.ds(0, OWN + 1)], packed.at[pl.ds(OWN + 1, OWN + 1)], across),
        send(1, logit.at[pl.ds(64, 64)], ext.at[pl.ds(0, 64)], after),
        send(2, logit.at[pl.ds(0, 64)], ext.at[pl.ds(192, 64)], before),
        send(3, target.at[pl.ds(96, RADIUS)], goal.at[pl.ds(0, RADIUS)], after),
        send(4, target.at[pl.ds(0, RADIUS)], goal.at[pl.ds(160, RADIUS)], before),
    ]

    def butterfly(value):
        real0, real1 = value[:FX, :128], value[:FX, 128:]
        imag0, imag1 = value[FX:, :128], value[FX:, 128:]
        even = jnp.concatenate([real0 + real1, imag0 + imag1], 1)
        odd = jnp.concatenate([real0 - real1, imag0 - imag1], 1)
        return even, odd

    def spectrum(group):
        base = group * (OWN + 1)
        ends = packed[base + OWN, 0:8, :]
        edge = edge_c[...]
        for k in range(OWN):
            taps = jnp.concatenate([packed[base + k], jnp.zeros((56, 128), F32)], 0)
            half_way = left_mul((taps_c[0], taps_c[1]), taps, dot_t)
            stacked = []
            for part_id in range(2):
                row = ends[2 * k + part_id : 2 * k + part_id + 1, :]
                own = half_way[NX * part_id : NX * (part_id + 1)] + edge * row
                stacked.append(jnp.concatenate([own[:FX], own[FX:]], 1))
            value = jnp.concatenate(stacked, 0)
            for odd in range(2):
                spec[group * OWN + k, :, 256 * odd : 256 * odd + 256] = right_mul(
                    value, (rows_c[odd, 0], rows_c[odd, 1]), dot
                )

    for load in loads[3:6]:
        load.wait()
    spectrum(0)

    for load in loads[6:9]:
        load.wait()
    sends[1].wait()
    sends[2].wait()
    row = lax.broadcasted_iota(jnp.int32, (NY, COLS), 0) - 64 + tile * BAND
    mask = jnp.where((row >= 0) & (row < tiles * BAND), jax.nn.sigmoid(3.0 * ext[...]), 0.0)
    even, odd = butterfly(left_mul((into_c[0], into_c[1]), mask, dot_t))
    mask_spec = (
        right_mul(even, (rows_c[0, 0], rows_c[0, 1]), dot),
        right_mul(odd, (rows_c[1, 0], rows_c[1, 1]), dot),
    )

    def forward(k):
        ends = []
        for odd in range(2):
            mr, mi = mask_spec[odd][:, :128], mask_spec[odd][:, 128:]
            rows = []
            for c in range(2):
                sr = spec[k, FX * c : FX * (c + 1), 256 * odd : 256 * odd + 128]
                si = spec[k, FX * c : FX * (c + 1), 256 * odd + 128 : 256 * odd + 256]
                rows.append(jnp.concatenate([sr * mr + si * mi, sr * mi - si * mr], 1))
            ends.append(right_mul(jnp.concatenate(rows, 0), (rows_c[odd, 0], rows_c[odd, 1]), dot_t))
        plus, minus = ends[0] + ends[1], ends[0] - ends[1]
        total = None
        for c in range(2):
            rows = slice(FX * c, FX * (c + 1))
            wave = jnp.concatenate(
                [
                    jnp.concatenate([plus[rows, :128], minus[rows, :128]], 1),
                    jnp.concatenate([plus[rows, 128:], minus[rows, 128:]], 1),
                ],
                0,
            )
            field = left_mul((out_c[0], out_c[1]), wave, dot)
            fields[2 * k + c] = field
            total = field * field if total is None else total + field * field
        return total

    inten = None
    for k in range(BOTH):
        if k == OWN:
            sends[0].wait()
            spectrum(1)
        own = forward(k)
        inten = own if inten is None else inten + own
    part[...] = inten
    swap = send(5, part, part_in, mate)

    sends[3].wait()
    sends[4].wait()
    for load in loads[9:]:
        load.wait()
    goal_t = dot_t(pick_c[...], goal[...].astype(F32).astype(BF16))

    swap.wait()
    printed = jax.nn.sigmoid(6.0 * (part[...] + part_in[...] - 1.0))
    goal_t = jnp.concatenate([goal_t, jnp.zeros((FIELD, NY - FROWS), F32)], 1)
    slope = 12.0 * (printed - goal_t) * printed * (1.0 - printed)
    lane = lax.broadcasted_iota(jnp.int32, (FIELD, NY), 1)
    place = lane - RADIUS + tile * BAND
    slope = jnp.where((lane < FROWS) & (place >= 0) & (place < tiles * BAND), slope, 0.0)

    acc = [None, None]
    for k in range(BOTH):
        evens, odds = [], []
        for c in range(2):
            source = slope * fields[2 * k + c]
            even, odd = butterfly(left_mul((back_c[0], back_c[1]), source, dot))
            evens.append(even)
            odds.append(odd)
        for odd, values in enumerate((evens, odds)):
            wave = right_mul(jnp.concatenate(values, 0), (rows_c[odd, 0], rows_c[odd, 1]), dot)
            for c in range(2):
                rows = slice(FX * c, FX * (c + 1))
                sr = spec[k, FX * c : FX * (c + 1), 256 * odd : 256 * odd + 128]
                si = spec[k, FX * c : FX * (c + 1), 256 * odd + 128 : 256 * odd + 256]
                gr, gi = wave[rows, :128], wave[rows, 128:]
                real, imag = sr * gr - si * gi, sr * gi + si * gr
                if acc[odd] is None:
                    acc[odd] = (real, imag)
                else:
                    acc[odd] = (acc[odd][0] + real, acc[odd][1] + imag)

    sign = 1.0 - 2.0 * lax.rem(lax.broadcasted_iota(jnp.int32, (FX, 128), 1), 2).astype(F32)
    even = jnp.concatenate([acc[0][0] * sign, acc[0][1] * sign], 1)
    odd = jnp.concatenate([-acc[1][1] * sign, acc[1][0] * sign], 1)
    back = right_mul(even, (rows_c[0, 0], rows_c[0, 1]), dot_t) + right_mul(odd, (rows_c[1, 0], rows_c[1, 1]), dot_t)
    back = jnp.concatenate([back[:, :128], back[:, 128:]], 0)
    grad[...] = left_mul((last_c[0], last_c[1]), back, dot)
    swap_2 = send(6, grad.at[pl.ds(64, 64)], grad_in, mate)

    own = jax.nn.sigmoid(3.0 * ext[64 : 64 + BAND, :])
    own = jnp.where(half == 0, own[:, :128], own[:, 128:])
    own = jnp.where(core == 0, own[:, :64], own[:, 64:])
    factor = 3.0 * own * (1.0 - own)
    swap_2.wait()
    total = grad[0:64, :] + grad_in[...]
    result[...] = jnp.transpose(total) * factor


def body(consts, mask_logit, target, kern_real, kern_imag, kern_weight):
    any_spec = pl.BlockSpec(memory_space=pl.ANY)
    vm = pltpu.VMEM
    scratch = [
        vm((NY, COLS), F32),
        vm((FROWS, COLS), jnp.int32),
        vm((OWN, TAPS, TAPS), F32),
        vm((OWN, TAPS, TAPS), F32),
        pltpu.SMEM((OWN,), F32),
        vm((2, 2 * NX, 128), BF16),
        vm((NX, 128), F32),
        vm((2, 2, 256, 256), BF16),
        vm((2, NX, COLS), BF16),
        vm((2, FIELD, NX), BF16),
        vm((FIELD, COLS), BF16),
        vm((2, NX, FIELD), BF16),
        vm((2, 128, NX), BF16),
        vm((2 * (OWN + 1), 72, 128), F32),
        vm((BOTH, 2 * FX, 512), F32),
        vm((2 * BOTH, FIELD, NY), F32),
        vm((FIELD, NY), F32),
        vm((FIELD, NY), F32),
        vm((128, BAND), F32),
        vm((64, BAND), F32),
        pltpu.SemaphoreType.DMA((13,)),
        pltpu.SemaphoreType.DMA((7,)),
        pltpu.SemaphoreType.DMA((7,)),
    ]
    return pl.pallas_call(
        kernel,
        out_shape=jax.ShapeDtypeStruct((BAND, 64), F32),
        in_specs=[any_spec] * (5 + len(NAMES)),
        out_specs=pl.BlockSpec(memory_space=pltpu.VMEM),
        scratch_shapes=scratch,
        compiler_params=pltpu.CompilerParams(
            collective_id=0, has_side_effects=True, vmem_limit_bytes=48 * 2**20
        ),
    )(mask_logit, target, kern_real, kern_imag, kern_weight, *consts)


def solution(mesh):
    made = tables()
    consts = [made[name] for name in NAMES]
    in_specs = (
        P("tile", None),
        P("tile", None),
        P("kern", None, None),
        P("kern", None, None),
        P("kern"),
    )
    mapped = jax.shard_map(
        lambda *args: body([jnp.asarray(c) for c in consts], *args),
        mesh=mesh, in_specs=in_specs, out_specs=P("tile", "kern"), check_vma=False,
    )
    return mapped
```

```python
import functools
import math

import jax
import jax.numpy as jnp
import ml_dtypes
import numpy as np
from jax import lax
from jax.experimental import pallas as pl
from jax.experimental.pallas import tpu as pltpu
from jax.sharding import PartitionSpec as P

F32 = jnp.float32
BF16 = jnp.bfloat16
MESH = pl.DeviceIdType.MESH

BAND = 128
COLS = 256
TAPS = 65
RADIUS = 32
OWN = 3
BOTH = 2 * OWN
NX = 224
FX = NX // 2
NY = 256
RUN = 16
PACK = 72 * OWN + 8
FIELD = 160
FROWS = 192


def pair(table):
    high = table.astype(ml_dtypes.bfloat16)
    low = (table - high.astype(np.float64)).astype(ml_dtypes.bfloat16)
    return np.stack([high, low])


def tables():
    theta = 2.0 * np.pi * (np.arange(FX) + 0.5) / NX

    def wave(offsets):
        angle = theta[:, None] * offsets[None, :]
        return np.concatenate([np.cos(angle), -np.sin(angle)], 0)

    scale = 2.0 / (NX * NY)
    into, back_in, out, last, pick = [], [], [], [], []
    for half in range(2):
        local = np.arange(COLS) - 64 * half
        full = wave(local) * ((local >= 0) & (local < 192))[None, :]
        into.append(pair(full))
        part = full[:, 96 * half : 96 * half + FIELD]
        back_in.append(pair(part))
        out.append(pair(scale * part.T))
        for core in range(2):
            cols = np.concatenate([64 * (2 * half + c) + np.arange(64) for c in (core, 1 - core)])
            last.append(pair(2.0 * scale * full[:, cols].T))
        pick.append((np.arange(COLS)[None, :] == np.arange(FIELD)[:, None] + 96 * half))
    taps = wave(np.arange(64) - RADIUS)
    zero = np.zeros_like(taps)
    taps = np.concatenate([np.concatenate([taps, zero], 1), np.concatenate([zero, taps], 1)], 0)
    edge = np.broadcast_to(wave(np.array([RADIUS])), (NX, 128))
    rows = []
    for odd in range(2):
        angle = 2.0 * np.pi * np.arange(128)[:, None] * (2 * np.arange(128) + odd)[None, :] / NY
        c, s = np.cos(angle), np.sin(angle)
        rows.append(pair(np.concatenate([np.concatenate([c, -s], 1), np.concatenate([s, c], 1)], 0)))
    return dict(
        rows=np.stack(rows),
        into=np.stack(into),
        taps=pair(taps),
        edge=edge.astype(np.float32),
        out=np.stack(out),
        back_in=np.stack(back_in),
        last=np.stack(last),
        pick=np.stack(pick).astype(ml_dtypes.bfloat16),
    )


NAMES = ("taps", "edge", "rows", "into", "out", "pick", "back_in", "last")


def split(value):
    high = value.astype(BF16)
    return high, (value - high.astype(F32)).astype(BF16)


def dot(left, right):
    return jnp.dot(left, right, preferred_element_type=F32)


def dot_t(left, right):
    return lax.dot_general(left, right, (((1,), (1,)), ((), ())), preferred_element_type=F32)


def right_mul(value, table, mul):
    high, low = split(value)
    count = value.shape[0]
    both = mul(jnp.concatenate([high, low], 0), table[0])
    return both[:count] + both[count:] + mul(high, table[1])


def left_mul(table, value, mul):
    high, low = split(value)
    return mul(table[0], high) + mul(table[1], high) + mul(table[0], low)


def kernel(
    logit, target, kern_real, kern_imag, weight, taps_h, edge_h, rows_h, into_h, out_h, pick_h, back_h, last_h,
    result,
    ext, goal, kr, ki, w, taps_c, edge_c, rows_c, into_c, out_c, pick_c, back_c, last_c,
    packed, spec, fields, part, part_in, grad, grad_in,
    local_sem, send_sem, recv_sem,
):
    tile, kern = lax.axis_index("tile"), lax.axis_index("kern")
    tiles = lax.axis_size("tile")
    half, core = kern // 2, lax.rem(kern, 2)
    before = {"tile": lax.rem(tile + tiles - 1, tiles)}
    after = {"tile": lax.rem(tile + 1, tiles)}
    mate = {"kern": 2 * half + (1 - core)}
    across = {"kern": 2 * (1 - half) + core}

    place = lax.rem(tile, RUN)
    head, tail = place == 0, place == RUN - 1
    turn_before = head & (tile > 0)
    turn_after = tail & (tile < tiles - 1)

    barrier = pltpu.get_barrier_semaphore()

    def greet(device):
        pl.semaphore_signal(barrier, inc=1, device_id=device, device_id_type=MESH)

    greet(across)
    greet(mate)
    pl.when(jnp.logical_not(tail))(lambda: greet(after))
    pl.when(jnp.logical_not(head))(lambda: greet(before))

    pairs = (
        (kern_real, kr),
        (kern_imag, ki),
        (weight, w),
        (taps_h, taps_c),
        (edge_h, edge_c),
        (rows_h, rows_c),
        (logit, ext.at[pl.ds(64, BAND)]),
        (into_h.at[half], into_c),
        (out_h.at[half], out_c),
        (target, goal.at[pl.ds(RADIUS, BAND)]),
        (pick_h.at[half], pick_c),
        (back_h.at[half], back_c),
        (last_h.at[kern], last_c),
    )
    loads = [pltpu.make_async_copy(src, dst, local_sem.at[i]) for i, (src, dst) in enumerate(pairs)]
    for load in loads:
        load.start()

    def send(index, src, dst, device):
        copy = pltpu.make_async_remote_copy(
            src_ref=src, dst_ref=dst, send_sem=send_sem.at[index], recv_sem=recv_sem.at[index],
            device_id=device, device_id_type=MESH,
        )
        return copy

    for load in loads[:3]:
        load.wait()
    eye = lax.broadcasted_iota(jnp.int32, (TAPS, 128), 0) == lax.broadcasted_iota(jnp.int32, (TAPS, 128), 1)
    ends = []
    for k in range(OWN):
        factor = jnp.sqrt(jnp.full((TAPS, TAPS), w[k], F32))
        real, imag = kr[k] * factor, ki[k] * factor
        packed[72 * k + 64 : 72 * k + 72, :] = jnp.zeros((8, 128), F32)
        packed[72 * k : 72 * k + TAPS, :] = jnp.concatenate([real[:, 0:64], imag[:, 0:64]], axis=1)
        for grid in (real, imag):
            column = jnp.broadcast_to(grid[:, 64:65], (TAPS, 128))
            ends.append(jnp.sum(jnp.where(eye, column, 0.0), axis=0, keepdims=True))
    row_id = lax.broadcasted_iota(jnp.int32, (8, 128), 0)
    end_rows = jnp.zeros((8, 128), F32)
    for i, end in enumerate(ends):
        end_rows = jnp.where(row_id == i, jnp.broadcast_to(end, (8, 128)), end_rows)
    packed[72 * OWN : 72 * OWN + 8, :] = end_rows

    ahead = jnp.where(tail, turn_after.astype(jnp.int32), 1)
    pl.semaphore_wait(barrier, 2 + jnp.where(head, 0, 1) + ahead)
    pl.when(turn_before)(lambda: greet(before))
    pl.when(turn_after)(lambda: greet(after))

    mask_down = send(0, logit.at[pl.ds(64, 64)], ext.at[pl.ds(0, 64)], after)
    mask_up = send(1, logit.at[pl.ds(0, 64)], ext.at[pl.ds(192, 64)], before)
    taps_over = send(2, packed.at[pl.ds(0, PACK)], packed.at[pl.ds(PACK, PACK)], across)
    goal_down = send(3, target.at[pl.ds(96, RADIUS)], goal.at[pl.ds(0, RADIUS)], after)
    goal_up = send(4, target.at[pl.ds(0, RADIUS)], goal.at[pl.ds(160, RADIUS)], before)
    has_before, has_after = tile > 0, tile < tiles - 1
    inner = jnp.logical_not(head)

    pl.when(has_after)(mask_down.start)
    pl.when(inner)(mask_up.start)
    taps_over.start()
    pl.when(has_after)(goal_down.start)
    pl.when(inner)(goal_up.start)

    def butterfly(value):
        real0, real1 = value[:FX, :128], value[:FX, 128:]
        imag0, imag1 = value[FX:, :128], value[FX:, 128:]
        even = jnp.concatenate([real0 + real1, imag0 + imag1], 1)
        odd = jnp.concatenate([real0 - real1, imag0 - imag1], 1)
        return even, odd

    def spectrum(group):
        base = group * PACK
        ends = packed[base + 72 * OWN : base + PACK, :]
        edge = edge_c[...]
        for k in range(OWN):
            taps = jnp.concatenate([packed[base + 72 * k : base + 72 * k + 72, :], jnp.zeros((56, 128), F32)], 0)
            half_way = left_mul((taps_c[0], taps_c[1]), taps, dot_t)
            stacked = []
            for part_id in range(2):
                row = ends[2 * k + part_id : 2 * k + part_id + 1, :]
                own = half_way[NX * part_id : NX * (part_id + 1)] + edge * row
                stacked.append(jnp.concatenate([own[:FX], own[FX:]], 1))
            value = jnp.concatenate(stacked, 0)
            for odd in range(2):
                spec[group * OWN + k, :, 256 * odd : 256 * odd + 256] = right_mul(
                    value, (rows_c[odd, 0], rows_c[odd, 1]), dot
                )

    for load in loads[3:6]:
        load.wait()
    spectrum(0)
    taps_over.wait_recv()
    spectrum(1)

    for load in loads[6:9]:
        load.wait()

    @pl.when(turn_before)
    def _():
        pl.semaphore_wait(barrier, 1)
        mask_up.start()
        goal_up.start()

    pl.when(has_before)(mask_down.wait_recv)
    pl.when(has_after)(mask_up.wait_recv)
    row = lax.broadcasted_iota(jnp.int32, (NY, COLS), 0) - 64 + tile * BAND
    mask = jnp.where((row >= 0) & (row < tiles * BAND), jax.nn.sigmoid(3.0 * ext[...]), 0.0)
    even, odd = butterfly(left_mul((into_c[0], into_c[1]), mask, dot_t))
    mask_spec = (
        right_mul(even, (rows_c[0, 0], rows_c[0, 1]), dot),
        right_mul(odd, (rows_c[1, 0], rows_c[1, 1]), dot),
    )

    def forward(k):
        ends = []
        for odd in range(2):
            mr, mi = mask_spec[odd][:, :128], mask_spec[odd][:, 128:]
            rows = []
            for c in range(2):
                sr = spec[k, FX * c : FX * (c + 1), 256 * odd : 256 * odd + 128]
                si = spec[k, FX * c : FX * (c + 1), 256 * odd + 128 : 256 * odd + 256]
                rows.append(jnp.concatenate([sr * mr + si * mi, sr * mi - si * mr], 1))
            ends.append(right_mul(jnp.concatenate(rows, 0), (rows_c[odd, 0], rows_c[odd, 1]), dot_t))
        plus, minus = ends[0] + ends[1], ends[0] - ends[1]
        total = None
        for c in range(2):
            rows = slice(FX * c, FX * (c + 1))
            wave = jnp.concatenate(
                [
                    jnp.concatenate([plus[rows, :128], minus[rows, :128]], 1),
                    jnp.concatenate([plus[rows, 128:], minus[rows, 128:]], 1),
                ],
                0,
            )
            field = left_mul((out_c[0], out_c[1]), wave, dot)
            fields[2 * k + c] = field
            total = field * field if total is None else total + field * field
        return total

    inten = None
    for k in range(BOTH):
        own = forward(k)
        inten = own if inten is None else inten + own
    part[...] = inten
    swap = send(5, part, part_in, mate)
    swap.start()

    pl.when(has_before)(goal_down.wait_recv)
    pl.when(has_after)(goal_up.wait_recv)
    for load in loads[9:]:
        load.wait()
    goal_t = dot_t(pick_c[...], goal[...].astype(F32).astype(BF16))

    swap.wait()
    printed = jax.nn.sigmoid(6.0 * (part[...] + part_in[...] - 1.0))
    goal_t = jnp.concatenate([goal_t, jnp.zeros((FIELD, NY - FROWS), F32)], 1)
    slope = 12.0 * (printed - goal_t) * printed * (1.0 - printed)
    lane = lax.broadcasted_iota(jnp.int32, (FIELD, NY), 1)
    line = lane - RADIUS + tile * BAND
    slope = jnp.where((lane < FROWS) & (line >= 0) & (line < tiles * BAND), slope, 0.0)

    acc = [None, None]
    for k in range(BOTH):
        evens, odds = [], []
        for c in range(2):
            source = slope * fields[2 * k + c]
            even, odd = butterfly(left_mul((back_c[0], back_c[1]), source, dot))
            evens.append(even)
            odds.append(odd)
        for odd, values in enumerate((evens, odds)):
            wave = right_mul(jnp.concatenate(values, 0), (rows_c[odd, 0], rows_c[odd, 1]), dot)
            for c in range(2):
                rows = slice(FX * c, FX * (c + 1))
                sr = spec[k, FX * c : FX * (c + 1), 256 * odd : 256 * odd + 128]
                si = spec[k, FX * c : FX * (c + 1), 256 * odd + 128 : 256 * odd + 256]
                gr, gi = wave[rows, :128], wave[rows, 128:]
                real, imag = sr * gr - si * gi, sr * gi + si * gr
                if acc[odd] is None:
                    acc[odd] = (real, imag)
                else:
                    acc[odd] = (acc[odd][0] + real, acc[odd][1] + imag)

    sign = 1.0 - 2.0 * lax.rem(lax.broadcasted_iota(jnp.int32, (FX, 128), 1), 2).astype(F32)
    even = jnp.concatenate([acc[0][0] * sign, acc[0][1] * sign], 1)
    odd = jnp.concatenate([-acc[1][1] * sign, acc[1][0] * sign], 1)
    back = right_mul(even, (rows_c[0, 0], rows_c[0, 1]), dot_t) + right_mul(odd, (rows_c[1, 0], rows_c[1, 1]), dot_t)
    back = jnp.concatenate([back[:, :128], back[:, 128:]], 0)
    grad[...] = left_mul((last_c[0], last_c[1]), back, dot)
    swap_2 = send(6, grad.at[pl.ds(64, 64)], grad_in, mate)
    swap_2.start()

    own = ext[64 : 64 + BAND, :]
    own = jnp.transpose(jnp.where(half == 0, own[:, :128], own[:, 128:]))
    own = jax.nn.sigmoid(3.0 * jnp.where(core == 0, own[:64], own[64:]))
    factor = 3.0 * own * (1.0 - own)
    swap_2.wait()
    result[...] = (grad[0:64, :] + grad_in[...]) * factor
    taps_over.wait_send()
    for copy in (mask_down, goal_down):
        pl.when(has_after)(copy.wait_send)
    for copy in (mask_up, goal_up):
        pl.when(has_before)(copy.wait_send)


def body(consts, mask_logit, target, kern_real, kern_imag, kern_weight):
    any_spec = pl.BlockSpec(memory_space=pltpu.HBM)
    vm = pltpu.VMEM
    scratch = [
        vm((NY, COLS), F32),
        vm((FROWS, COLS), jnp.int32),
        vm((OWN, TAPS, TAPS), F32),
        vm((OWN, TAPS, TAPS), F32),
        pltpu.SMEM((OWN,), F32),
        vm((2, 2 * NX, 128), BF16),
        vm((NX, 128), F32),
        vm((2, 2, 256, 256), BF16),
        vm((2, NX, COLS), BF16),
        vm((2, FIELD, NX), BF16),
        vm((FIELD, COLS), BF16),
        vm((2, NX, FIELD), BF16),
        vm((2, 128, NX), BF16),
        vm((2 * PACK, 128), F32),
        vm((BOTH, 2 * FX, 512), F32),
        vm((2 * BOTH, FIELD, NY), F32),
        vm((FIELD, NY), F32),
        vm((FIELD, NY), F32),
        vm((128, BAND), F32),
        vm((64, BAND), F32),
        pltpu.SemaphoreType.DMA((13,)),
        pltpu.SemaphoreType.DMA((7,)),
        pltpu.SemaphoreType.DMA((7,)),
    ]
    total = pl.pallas_call(
        kernel,
        out_shape=pltpu.VMEM((64, BAND), F32),
        in_specs=[any_spec] * (5 + len(NAMES)),
        out_specs=pl.BlockSpec(memory_space=pltpu.VMEM),
        scratch_shapes=scratch,
        compiler_params=pltpu.CompilerParams(
            collective_id=0, has_side_effects=True, vmem_limit_bytes=48 * 2**20
        ),
    )(*[pltpu.with_memory_space_constraint(v, pltpu.HBM) for v in (mask_logit, target, kern_real, kern_imag, kern_weight, *consts)])
    return total.T


def solution(mesh):
    made = tables()
    consts = [made[name] for name in NAMES]
    in_specs = (
        P("tile", None),
        P("tile", None),
        P("kern", None, None),
        P("kern", None, None),
        P("kern"),
    )
    mapped = jax.shard_map(
        lambda *args: body([jnp.asarray(c) for c in consts], *args),
        mesh=mesh, in_specs=in_specs, out_specs=P("tile", "kern"), check_vma=False,
    )
    return mapped
```

```python
import functools
import math

import jax
import jax.numpy as jnp
import ml_dtypes
import numpy as np
from jax import lax
from jax.experimental import pallas as pl
from jax.experimental.pallas import tpu as pltpu
from jax.sharding import PartitionSpec as P

F32 = jnp.float32
BF16 = jnp.bfloat16
MESH = pl.DeviceIdType.MESH

BAND = 128
COLS = 256
TAPS = 65
RADIUS = 32
OWN = 3
BOTH = 2 * OWN
NX = 224
FX = NX // 2
NY = 256
RUN = 16
PACK = 72 * OWN + 8
FIELD = 160
FROWS = 192


def pair(table):
    high = table.astype(ml_dtypes.bfloat16)
    low = (table - high.astype(np.float64)).astype(ml_dtypes.bfloat16)
    return np.stack([high, low])


def tables():
    theta = 2.0 * np.pi * (np.arange(FX) + 0.5) / NX

    def wave(offsets):
        angle = theta[:, None] * offsets[None, :]
        return np.concatenate([np.cos(angle), -np.sin(angle)], 0)

    scale = 2.0 / (NX * NY)
    into, back_in, out, last, pick = [], [], [], [], []
    for half in range(2):
        local = np.arange(COLS) - 64 * half
        full = wave(local) * ((local >= 0) & (local < 192))[None, :]
        into.append(pair(full))
        part = full[:, 96 * half : 96 * half + FIELD]
        back_in.append(pair(part))
        out.append(pair(scale * part.T))
        for core in range(2):
            cols = np.concatenate([64 * (2 * half + c) + np.arange(64) for c in (core, 1 - core)])
            last.append(pair(2.0 * scale * full[:, cols].T))
        pick.append((np.arange(COLS)[None, :] == np.arange(FIELD)[:, None] + 96 * half))
    taps = wave(np.arange(64) - RADIUS)
    zero = np.zeros_like(taps)
    taps = np.concatenate([np.concatenate([taps, zero], 1), np.concatenate([zero, taps], 1)], 0)
    edge = np.broadcast_to(wave(np.array([RADIUS])), (NX, 128))
    rows = []
    for odd in range(2):
        angle = 2.0 * np.pi * np.arange(128)[:, None] * (2 * np.arange(128) + odd)[None, :] / NY
        c, s = np.cos(angle), np.sin(angle)
        rows.append(pair(np.concatenate([np.concatenate([c, -s], 1), np.concatenate([s, c], 1)], 0)))
    return dict(
        rows=np.stack(rows),
        into=np.stack(into),
        taps=pair(taps),
        edge=edge.astype(np.float32),
        out=np.stack(out),
        back_in=np.stack(back_in),
        last=np.stack(last),
        pick=np.stack(pick).astype(ml_dtypes.bfloat16),
    )


NAMES = ("taps", "edge", "rows", "into", "out", "pick", "back_in", "last")


def split(value):
    high = value.astype(BF16)
    return high, (value - high.astype(F32)).astype(BF16)


def dot(left, right):
    return jnp.dot(left, right, preferred_element_type=F32)


def dot_t(left, right):
    return lax.dot_general(left, right, (((1,), (1,)), ((), ())), preferred_element_type=F32)


def right_mul(value, table, mul):
    high, low = split(value)
    count = value.shape[0]
    both = mul(jnp.concatenate([high, low], 0), table[0])
    return both[:count] + both[count:] + mul(high, table[1])


def left_mul(table, value, mul):
    high, low = split(value)
    return mul(table[0], high) + mul(table[1], high) + mul(table[0], low)


def kernel(
    logit, target, kern_real, kern_imag, weight, taps_h, edge_h, rows_h, into_h, out_h, pick_h, back_h, last_h,
    result,
    ext, goal, kr, ki, w, taps_c, edge_c, rows_c, into_c, out_c, pick_c, back_c, last_c,
    packed, spec, fields, part, part_in, grad, grad_in,
    local_sem, send_sem, recv_sem, relay,
):
    tile, kern = lax.axis_index("tile"), lax.axis_index("kern")
    tiles = lax.axis_size("tile")
    half, core = kern // 2, lax.rem(kern, 2)
    before = {"tile": lax.rem(tile + tiles - 1, tiles)}
    after = {"tile": lax.rem(tile + 1, tiles)}
    mate = {"kern": 2 * half + (1 - core)}
    across = {"kern": 2 * (1 - half) + core}

    place = lax.rem(tile, RUN)
    head, tail = place == 0, place == RUN - 1
    eve = place == RUN - 2
    turn_before = head & (tile > 0)
    turn_after = tail & (tile < tiles - 1)

    barrier = pltpu.get_barrier_semaphore()

    def greet(device):
        pl.semaphore_signal(barrier, inc=1, device_id=device, device_id_type=MESH)

    inner = jnp.logical_not(tail)

    @pl.when(inner)
    def _():
        greet(across)
        greet(mate)

    pl.when(inner & jnp.logical_not(eve))(lambda: greet(after))
    pl.when(inner & jnp.logical_not(head))(lambda: greet(before))

    pairs = (
        (kern_real, kr),
        (kern_imag, ki),
        (weight, w),
        (taps_h, taps_c),
        (edge_h, edge_c),
        (rows_h, rows_c),
        (logit, ext.at[pl.ds(64, BAND)]),
        (into_h.at[half], into_c),
        (out_h.at[half], out_c),
        (target, goal.at[pl.ds(RADIUS, BAND)]),
        (pick_h.at[half], pick_c),
        (back_h.at[half], back_c),
        (last_h.at[kern], last_c),
    )
    def send(index, src, dst, device):
        return pltpu.make_async_remote_copy(
            src_ref=src, dst_ref=dst, send_sem=send_sem.at[index], recv_sem=recv_sem.at[index],
            device_id=device, device_id_type=MESH,
        )

    mask_down = send(0, logit.at[pl.ds(64, 64)], ext.at[pl.ds(0, 64)], after)
    mask_up = send(1, logit.at[pl.ds(0, 64)], ext.at[pl.ds(192, 64)], before)
    taps_over = send(2, packed.at[pl.ds(0, PACK)], packed.at[pl.ds(PACK, PACK)], across)
    goal_down = send(3, target.at[pl.ds(96, RADIUS)], goal.at[pl.ds(0, RADIUS)], after)
    goal_up = send(4, target.at[pl.ds(0, RADIUS)], goal.at[pl.ds(160, RADIUS)], before)
    has_before, has_after = tile > 0, tile < tiles - 1

    @pl.when(turn_after)
    def _():
        pl.semaphore_wait(barrier, 1)
        mask_down.start()
        goal_down.start()
        greet(after)

    pl.when(tail)(lambda: greet(before))

    loads = [pltpu.make_async_copy(src, dst, local_sem.at[i]) for i, (src, dst) in enumerate(pairs)]
    for load in loads:
        load.start()

    for load in loads[:3]:
        load.wait()
    eye = lax.broadcasted_iota(jnp.int32, (TAPS, 128), 0) == lax.broadcasted_iota(jnp.int32, (TAPS, 128), 1)
    ends = []
    for k in range(OWN):
        factor = jnp.sqrt(jnp.full((TAPS, TAPS), w[k], F32))
        real, imag = kr[k] * factor, ki[k] * factor
        packed[72 * k + 64 : 72 * k + 72, :] = jnp.zeros((8, 128), F32)
        packed[72 * k : 72 * k + TAPS, :] = jnp.concatenate([real[:, 0:64], imag[:, 0:64]], axis=1)
        for grid in (real, imag):
            column = jnp.broadcast_to(grid[:, 64:65], (TAPS, 128))
            ends.append(jnp.sum(jnp.where(eye, column, 0.0), axis=0, keepdims=True))
    row_id = lax.broadcasted_iota(jnp.int32, (8, 128), 0)
    end_rows = jnp.zeros((8, 128), F32)
    for i, end in enumerate(ends):
        end_rows = jnp.where(row_id == i, jnp.broadcast_to(end, (8, 128)), end_rows)
    packed[72 * OWN : 72 * OWN + 8, :] = end_rows

    @pl.when(inner)
    def _():
        pl.semaphore_wait(barrier, 3 + jnp.where(head, 0, 1))
        pl.when(turn_before)(lambda: greet(before))
        mask_down.start()
        pl.when(jnp.logical_not(head))(mask_up.start)
        taps_over.start()
        goal_down.start()
        pl.when(jnp.logical_not(head))(goal_up.start)

    @pl.when(eve)
    def _():
        for device in (across, mate):
            pl.semaphore_signal(relay, inc=1, device_id=device, device_id_type=MESH)
        pl.semaphore_wait(relay, 2)
        greet(after)

    def butterfly(value):
        real0, real1 = value[:FX, :128], value[:FX, 128:]
        imag0, imag1 = value[FX:, :128], value[FX:, 128:]
        even = jnp.concatenate([real0 + real1, imag0 + imag1], 1)
        odd = jnp.concatenate([real0 - real1, imag0 - imag1], 1)
        return even, odd

    def spectrum(group):
        base = group * PACK
        ends = packed[base + 72 * OWN : base + PACK, :]
        edge = edge_c[...]
        for k in range(OWN):
            taps = jnp.concatenate([packed[base + 72 * k : base + 72 * k + 72, :], jnp.zeros((56, 128), F32)], 0)
            half_way = left_mul((taps_c[0], taps_c[1]), taps, dot_t)
            stacked = []
            for part_id in range(2):
                row = ends[2 * k + part_id : 2 * k + part_id + 1, :]
                own = half_way[NX * part_id : NX * (part_id + 1)] + edge * row
                stacked.append(jnp.concatenate([own[:FX], own[FX:]], 1))
            value = jnp.concatenate(stacked, 0)
            for odd in range(2):
                spec[group * OWN + k, :, 256 * odd : 256 * odd + 256] = right_mul(
                    value, (rows_c[odd, 0], rows_c[odd, 1]), dot
                )

    for load in loads[3:6]:
        load.wait()
    spectrum(0)

    @pl.when(tail)
    def _():
        pl.semaphore_wait(barrier, 1)
        mask_up.start()
        taps_over.start()
        goal_up.start()

    taps_over.wait_recv()
    spectrum(1)

    for load in loads[6:9]:
        load.wait()

    @pl.when(turn_before)
    def _():
        pl.semaphore_wait(barrier, 1)
        mask_up.start()
        goal_up.start()

    pl.when(has_before)(mask_down.wait_recv)
    pl.when(has_after)(mask_up.wait_recv)
    row = lax.broadcasted_iota(jnp.int32, (NY, COLS), 0) - 64 + tile * BAND
    mask = jnp.where((row >= 0) & (row < tiles * BAND), jax.nn.sigmoid(3.0 * ext[...]), 0.0)
    even, odd = butterfly(left_mul((into_c[0], into_c[1]), mask, dot_t))
    mask_spec = (
        right_mul(even, (rows_c[0, 0], rows_c[0, 1]), dot),
        right_mul(odd, (rows_c[1, 0], rows_c[1, 1]), dot),
    )

    def forward(k):
        ends = []
        for odd in range(2):
            mr, mi = mask_spec[odd][:, :128], mask_spec[odd][:, 128:]
            rows = []
            for c in range(2):
                sr = spec[k, FX * c : FX * (c + 1), 256 * odd : 256 * odd + 128]
                si = spec[k, FX * c : FX * (c + 1), 256 * odd + 128 : 256 * odd + 256]
                rows.append(jnp.concatenate([sr * mr + si * mi, sr * mi - si * mr], 1))
            ends.append(right_mul(jnp.concatenate(rows, 0), (rows_c[odd, 0], rows_c[odd, 1]), dot_t))
        plus, minus = ends[0] + ends[1], ends[0] - ends[1]
        total = None
        for c in range(2):
            rows = slice(FX * c, FX * (c + 1))
            wave = jnp.concatenate(
                [
                    jnp.concatenate([plus[rows, :128], minus[rows, :128]], 1),
                    jnp.concatenate([plus[rows, 128:], minus[rows, 128:]], 1),
                ],
                0,
            )
            field = left_mul((out_c[0], out_c[1]), wave, dot)
            fields[2 * k + c] = field
            total = field * field if total is None else total + field * field
        return total

    inten = None
    for k in range(BOTH):
        own = forward(k)
        inten = own if inten is None else inten + own
    part[...] = inten
    swap = send(5, part, part_in, mate)
    swap.start()

    pl.when(has_before)(goal_down.wait_recv)
    pl.when(has_after)(goal_up.wait_recv)
    for load in loads[9:]:
        load.wait()
    goal_t = dot_t(pick_c[...], goal[...].astype(F32).astype(BF16))

    swap.wait()
    printed = jax.nn.sigmoid(6.0 * (part[...] + part_in[...] - 1.0))
    goal_t = jnp.concatenate([goal_t, jnp.zeros((FIELD, NY - FROWS), F32)], 1)
    slope = 12.0 * (printed - goal_t) * printed * (1.0 - printed)
    lane = lax.broadcasted_iota(jnp.int32, (FIELD, NY), 1)
    line = lane - RADIUS + tile * BAND
    slope = jnp.where((lane < FROWS) & (line >= 0) & (line < tiles * BAND), slope, 0.0)

    acc = [None, None]
    for k in range(BOTH):
        evens, odds = [], []
        for c in range(2):
            source = slope * fields[2 * k + c]
            even, odd = butterfly(left_mul((back_c[0], back_c[1]), source, dot))
            evens.append(even)
            odds.append(odd)
        for odd, values in enumerate((evens, odds)):
            wave = right_mul(jnp.concatenate(values, 0), (rows_c[odd, 0], rows_c[odd, 1]), dot)
            for c in range(2):
                rows = slice(FX * c, FX * (c + 1))
                sr = spec[k, FX * c : FX * (c + 1), 256 * odd : 256 * odd + 128]
                si = spec[k, FX * c : FX * (c + 1), 256 * odd + 128 : 256 * odd + 256]
                gr, gi = wave[rows, :128], wave[rows, 128:]
                real, imag = sr * gr - si * gi, sr * gi + si * gr
                if acc[odd] is None:
                    acc[odd] = (real, imag)
                else:
                    acc[odd] = (acc[odd][0] + real, acc[odd][1] + imag)

    sign = 1.0 - 2.0 * lax.rem(lax.broadcasted_iota(jnp.int32, (FX, 128), 1), 2).astype(F32)
    even = jnp.concatenate([acc[0][0] * sign, acc[0][1] * sign], 1)
    odd = jnp.concatenate([-acc[1][1] * sign, acc[1][0] * sign], 1)
    back = right_mul(even, (rows_c[0, 0], rows_c[0, 1]), dot_t) + right_mul(odd, (rows_c[1, 0], rows_c[1, 1]), dot_t)
    back = jnp.concatenate([back[:, :128], back[:, 128:]], 0)
    grad[...] = left_mul((last_c[0], last_c[1]), back, dot)
    swap_2 = send(6, grad.at[pl.ds(64, 64)], grad_in, mate)
    swap_2.start()

    own = ext[64 : 64 + BAND, :]
    own = jnp.transpose(jnp.where(half == 0, own[:, :128], own[:, 128:]))
    own = jax.nn.sigmoid(3.0 * jnp.where(core == 0, own[:64], own[64:]))
    factor = 3.0 * own * (1.0 - own)
    swap_2.wait()
    result[...] = (grad[0:64, :] + grad_in[...]) * factor
    taps_over.wait_send()
    for copy in (mask_down, goal_down):
        pl.when(has_after)(copy.wait_send)
    for copy in (mask_up, goal_up):
        pl.when(has_before)(copy.wait_send)


def body(consts, mask_logit, target, kern_real, kern_imag, kern_weight):
    any_spec = pl.BlockSpec(memory_space=pltpu.HBM)
    vm = pltpu.VMEM
    scratch = [
        vm((NY, COLS), F32),
        vm((FROWS, COLS), jnp.int32),
        vm((OWN, TAPS, TAPS), F32),
        vm((OWN, TAPS, TAPS), F32),
        pltpu.SMEM((OWN,), F32),
        vm((2, 2 * NX, 128), BF16),
        vm((NX, 128), F32),
        vm((2, 2, 256, 256), BF16),
        vm((2, NX, COLS), BF16),
        vm((2, FIELD, NX), BF16),
        vm((FIELD, COLS), BF16),
        vm((2, NX, FIELD), BF16),
        vm((2, 128, NX), BF16),
        vm((2 * PACK, 128), F32),
        vm((BOTH, 2 * FX, 512), F32),
        vm((2 * BOTH, FIELD, NY), F32),
        vm((FIELD, NY), F32),
        vm((FIELD, NY), F32),
        vm((128, BAND), F32),
        vm((64, BAND), F32),
        pltpu.SemaphoreType.DMA((13,)),
        pltpu.SemaphoreType.DMA((7,)),
        pltpu.SemaphoreType.DMA((7,)),
        pltpu.SemaphoreType.REGULAR,
    ]
    total = pl.pallas_call(
        kernel,
        out_shape=pltpu.VMEM((64, BAND), F32),
        in_specs=[any_spec] * (5 + len(NAMES)),
        out_specs=pl.BlockSpec(memory_space=pltpu.VMEM),
        scratch_shapes=scratch,
        compiler_params=pltpu.CompilerParams(
            collective_id=0, has_side_effects=True, vmem_limit_bytes=48 * 2**20
        ),
    )(*[pltpu.with_memory_space_constraint(v, pltpu.HBM) for v in (mask_logit, target, kern_real, kern_imag, kern_weight, *consts)])
    return total.T


def solution(mesh):
    made = tables()
    consts = [made[name] for name in NAMES]
    in_specs = (
        P("tile", None),
        P("tile", None),
        P("kern", None, None),
        P("kern", None, None),
        P("kern"),
    )
    mapped = jax.shard_map(
        lambda *args: body([jnp.asarray(c) for c in consts], *args),
        mesh=mesh, in_specs=in_specs, out_specs=P("tile", "kern"), check_vma=False,
    )
    return mapped
```

```python
import functools
import math

import jax
import jax.numpy as jnp
import ml_dtypes
import numpy as np
from jax import lax
from jax.experimental import pallas as pl
from jax.experimental.pallas import tpu as pltpu
from jax.sharding import PartitionSpec as P

F32 = jnp.float32
BF16 = jnp.bfloat16
MESH = pl.DeviceIdType.MESH

BAND = 128
COLS = 256
TAPS = 65
RADIUS = 32
OWN = 3
BOTH = 2 * OWN
NX = 224
FX = NX // 2
NY = 256
RUN = 16
PACK = 72 * OWN + 8
FIELD = 160
FROWS = 192


def triple(table, axis, order):
    high = table.astype(ml_dtypes.bfloat16)
    low = (table - high.astype(np.float64)).astype(ml_dtypes.bfloat16)
    return np.concatenate([(high, low)[i] for i in order], axis)


LEFT = (0, 1, 0)
RIGHT = (0, 0, 1)


def tables():
    theta = 2.0 * np.pi * (np.arange(FX) + 0.5) / NX

    def wave(offsets):
        angle = theta[:, None] * offsets[None, :]
        return np.concatenate([np.cos(angle), -np.sin(angle)], 0)

    scale = 2.0 / (NX * NY)
    into, back_in, out, last, pick = [], [], [], [], []
    for half in range(2):
        local = np.arange(COLS) - 64 * half
        full = wave(local) * ((local >= 0) & (local < 192))[None, :]
        into.append(triple(full, 1, LEFT))
        part = full[:, 96 * half : 96 * half + FIELD]
        back_in.append(triple(part, 1, LEFT))
        out.append(triple(scale * part.T, 1, LEFT))
        for core in range(2):
            cols = np.concatenate([64 * (2 * half + c) + np.arange(64) for c in (core, 1 - core)])
            last.append(triple(2.0 * scale * full[:, cols].T, 1, LEFT))
        pick.append((np.arange(COLS)[None, :] == np.arange(FIELD)[:, None] + 96 * half))
    taps = wave(np.arange(64) - RADIUS)
    zero = np.zeros_like(taps)
    taps = np.concatenate([np.concatenate([taps, zero], 1), np.concatenate([zero, taps], 1)], 0)
    edge = np.broadcast_to(wave(np.array([RADIUS])), (NX, 128))
    rows, rows_t = [], []
    for odd in range(2):
        angle = 2.0 * np.pi * np.arange(128)[:, None] * (2 * np.arange(128) + odd)[None, :] / NY
        c, s = np.cos(angle), np.sin(angle)
        table = np.concatenate([np.concatenate([c, -s], 1), np.concatenate([s, c], 1)], 0)
        rows.append(triple(table, 0, RIGHT))
        rows_t.append(triple(table.T, 0, RIGHT))
    return dict(
        rows=np.stack(rows),
        rows_t=np.stack(rows_t),
        into=np.stack(into),
        taps=triple(taps, 1, LEFT),
        edge=edge.astype(np.float32),
        out=np.stack(out),
        back_in=np.stack(back_in),
        last=np.stack(last),
        pick=np.stack(pick).astype(ml_dtypes.bfloat16),
    )


NAMES = ("taps", "edge", "rows", "rows_t", "into", "out", "pick", "back_in", "last")


def split(value):
    high = value.astype(BF16)
    return high, (value - high.astype(F32)).astype(BF16)


def dot(left, right):
    return jnp.dot(left, right, preferred_element_type=F32)


def dot_t(left, right):
    return lax.dot_general(left, right, (((1,), (1,)), ((), ())), preferred_element_type=F32)


def spread(value):
    high, low = split(value)
    return jnp.concatenate([high, low, high], 1)


def right_mul(value, table):
    return dot(spread(value), table)


def heap(value, axis=0):
    high, low = split(value)
    return jnp.concatenate([high, high, low], axis)


def left_mul(table, value, mul=dot):
    return mul(table, heap(value, 1 if mul is dot_t else 0))


def kernel(
    logit, target, kern_real, kern_imag, weight, taps_h, edge_h, rows_h, rows_t_h, into_h, out_h, pick_h, back_h, last_h,
    result,
    ext, goal, kr, ki, w, taps_c, edge_c, rows_c, rows_t_c, into_c, out_c, pick_c, back_c, last_c,
    packed, spec, streams, waves, near, far, packs, begun, ended, part, part_in, grad, grad_in,
    local_sem, send_sem, recv_sem, relay,
):
    tile, kern = lax.axis_index("tile"), lax.axis_index("kern")
    tiles = lax.axis_size("tile")
    half, core = kern // 2, lax.rem(kern, 2)
    before = {"tile": lax.rem(tile + tiles - 1, tiles)}
    after = {"tile": lax.rem(tile + 1, tiles)}
    mate = {"kern": 2 * half + (1 - core)}
    across = {"kern": 2 * (1 - half) + core}

    place = lax.rem(tile, RUN)
    head, tail = place == 0, place == RUN - 1
    eve = place == RUN - 2
    turn_before = head & (tile > 0)
    turn_after = tail & (tile < tiles - 1)

    barrier = pltpu.get_barrier_semaphore()

    def greet(device):
        pl.semaphore_signal(barrier, inc=1, device_id=device, device_id_type=MESH)

    inner = jnp.logical_not(tail)

    @pl.when(inner)
    def _():
        greet(across)
        greet(mate)

    pl.when(inner & jnp.logical_not(eve))(lambda: greet(after))
    pl.when(inner & jnp.logical_not(head))(lambda: greet(before))

    pairs = (
        (kern_real, kr),
        (kern_imag, ki),
        (weight, w),
        (taps_h, taps_c),
        (edge_h, edge_c),
        (rows_h, rows_c),
        (rows_t_h, rows_t_c),
        (logit, ext.at[pl.ds(64, BAND)]),
        (into_h.at[half], into_c),
        (out_h.at[half], out_c),
        (target, goal.at[pl.ds(RADIUS, BAND)]),
        (pick_h.at[half], pick_c),
        (back_h.at[half], back_c),
        (last_h.at[kern], last_c),
    )
    def send(index, src, dst, device):
        return pltpu.make_async_remote_copy(
            src_ref=src, dst_ref=dst, send_sem=send_sem.at[index], recv_sem=recv_sem.at[index],
            device_id=device, device_id_type=MESH,
        )

    mask_down = send(0, logit.at[pl.ds(64, 64)], ext.at[pl.ds(0, 64)], after)
    mask_up = send(1, logit.at[pl.ds(0, 64)], ext.at[pl.ds(192, 64)], before)
    taps_over = send(2, packed.at[pl.ds(0, PACK)], packed.at[pl.ds(PACK, PACK)], across)
    goal_down = send(3, target.at[pl.ds(96, RADIUS)], goal.at[pl.ds(0, RADIUS)], after)
    goal_up = send(4, target.at[pl.ds(0, RADIUS)], goal.at[pl.ds(160, RADIUS)], before)
    has_before, has_after = tile > 0, tile < tiles - 1

    @pl.when(turn_after)
    def _():
        pl.semaphore_wait(barrier, 1)
        mask_down.start()
        goal_down.start()
        greet(after)

    pl.when(tail)(lambda: greet(before))

    loads = [pltpu.make_async_copy(src, dst, local_sem.at[i]) for i, (src, dst) in enumerate(pairs)]
    for load in loads:
        load.start()

    for load in loads[:3]:
        load.wait()
    eye = lax.broadcasted_iota(jnp.int32, (TAPS, 128), 0) == lax.broadcasted_iota(jnp.int32, (TAPS, 128), 1)
    ends = []
    for k in range(OWN):
        factor = jnp.sqrt(jnp.full((TAPS, TAPS), w[k], F32))
        real, imag = kr[k] * factor, ki[k] * factor
        packed[72 * k + 64 : 72 * k + 72, :] = jnp.zeros((8, 128), F32)
        packed[72 * k : 72 * k + TAPS, :] = jnp.concatenate([real[:, 0:64], imag[:, 0:64]], axis=1)
        for grid in (real, imag):
            column = jnp.broadcast_to(grid[:, 64:65], (TAPS, 128))
            ends.append(jnp.sum(jnp.where(eye, column, 0.0), axis=0, keepdims=True))
    row_id = lax.broadcasted_iota(jnp.int32, (8, 128), 0)
    end_rows = jnp.zeros((8, 128), F32)
    for i, end in enumerate(ends):
        end_rows = jnp.where(row_id == i, jnp.broadcast_to(end, (8, 128)), end_rows)
    packed[72 * OWN : 72 * OWN + 8, :] = end_rows

    @pl.when(inner)
    def _():
        pl.semaphore_wait(barrier, 3 + jnp.where(head, 0, 1))
        pl.when(turn_before)(lambda: greet(before))
        mask_down.start()
        pl.when(jnp.logical_not(head))(mask_up.start)
        taps_over.start()
        goal_down.start()
        pl.when(jnp.logical_not(head))(goal_up.start)

    @pl.when(eve)
    def _():
        for device in (across, mate):
            pl.semaphore_signal(relay, inc=1, device_id=device, device_id_type=MESH)
        pl.semaphore_wait(relay, 2)
        greet(after)

    def butterfly(value):
        real0, real1 = value[:FX, :128], value[:FX, 128:]
        imag0, imag1 = value[FX:, :128], value[FX:, 128:]
        even = jnp.concatenate([real0 + real1, imag0 + imag1], 1)
        odd = jnp.concatenate([real0 - real1, imag0 - imag1], 1)
        return even, odd

    def spectrum(group):
        base = group * PACK
        ends = packed[base + 72 * OWN : base + PACK, :]
        edge = edge_c[...]
        for k in range(OWN):
            taps = jnp.concatenate([packed[base + 72 * k : base + 72 * k + 72, :], jnp.zeros((56, 128), F32)], 0)
            half_way = left_mul(taps_c[...], taps, dot_t)
            for c in range(2):
                row = ends[2 * k + c : 2 * k + c + 1, :]
                own = half_way[NX * c : NX * (c + 1)] + edge * row
                streams[0, k, FX * c : FX * (c + 1), :] = spread(jnp.concatenate([own[:FX], own[FX:]], 1))
        for odd in range(2):
            for k in range(OWN):
                spec[group * OWN + k, :, 256 * odd : 256 * odd + 256] = dot(streams[0, k], rows_c[odd])

    for load in loads[3:6]:
        load.wait()
    spectrum(0)

    @pl.when(tail)
    def _():
        pl.semaphore_wait(barrier, 1)
        mask_up.start()
        taps_over.start()
        goal_up.start()

    taps_over.wait_recv()
    spectrum(1)

    for load in loads[6:10]:
        load.wait()

    @pl.when(turn_before)
    def _():
        pl.semaphore_wait(barrier, 1)
        mask_up.start()
        goal_up.start()

    pl.when(has_before)(mask_down.wait_recv)
    pl.when(has_after)(mask_up.wait_recv)
    row = lax.broadcasted_iota(jnp.int32, (NY, COLS), 0) - 64 + tile * BAND
    mask = jnp.where((row >= 0) & (row < tiles * BAND), jax.nn.sigmoid(3.0 * ext[...]), 0.0)
    even, odd = butterfly(left_mul(into_c[...], mask, dot_t))
    mask_spec = (
        right_mul(even, rows_c[0]),
        right_mul(odd, rows_c[1]),
    )

    first_half = lax.broadcasted_iota(jnp.int32, (1, 128), 1) < 64

    def halves(left, right):
        return jnp.where(first_half, left, pltpu.roll(right, 64, 1))

    def square(field):
        return field[:, :128] * field[:, :128] + field[:, 128:] * field[:, 128:]

    total, tails = None, []
    for k in range(BOTH):
        for odd in range(2):
            mr, mi = mask_spec[odd][:, :128], mask_spec[odd][:, 128:]
            for c in range(2):
                sr = spec[k, FX * c : FX * (c + 1), 256 * odd : 256 * odd + 128]
                si = spec[k, FX * c : FX * (c + 1), 256 * odd + 128 : 256 * odd + 256]
                streams[odd, k, FX * c : FX * (c + 1), :] = spread(
                    jnp.concatenate([sr * mr + si * mi, sr * mi - si * mr], 1)
                )
    for k in range(BOTH):
        ends = [dot(streams[odd, k], rows_t_c[odd]) for odd in range(2)]
        plus, minus = ends[0] + ends[1], ends[0] - ends[1]
        plus_c = [jnp.concatenate([plus[FX * c : FX * (c + 1), :128], plus[FX * c : FX * (c + 1), 128:]], 0) for c in (0, 1)]
        minus_c = [jnp.concatenate([minus[FX * c : FX * (c + 1), :128], minus[FX * c : FX * (c + 1), 128:]], 0) for c in (0, 1)]
        waves[k] = heap(jnp.concatenate(plus_c, 1))
        packs[k] = halves(*minus_c)
    for k in range(BOTH):
        field = dot(out_c[...], waves[k])
        near[k] = field
        total = square(field) if total is None else total + square(field)
    part[0] = total
    swap_near = send(5, part.at[0], part_in.at[0], mate)
    swap_near.start()
    total = None
    for k in range(BOTH // 2):
        field = left_mul(out_c[...], jnp.concatenate([packs[2 * k], packs[2 * k + 1]], 1), dot)
        far[k] = field
        total = square(field) if total is None else total + square(field)
    part[1] = total + pltpu.roll(total, 64, 1)
    swap_far = send(7, part.at[1], part_in.at[1], mate)
    swap_far.start()

    pl.when(has_before)(goal_down.wait_recv)
    pl.when(has_after)(goal_up.wait_recv)
    for load in loads[10:]:
        load.wait()
    goal_t = dot_t(pick_c[...], goal[...].astype(F32).astype(BF16))
    goal_far = goal_t[:, 128:]
    goal_far = jnp.concatenate([goal_far, goal_far], 1)

    lane = lax.broadcasted_iota(jnp.int32, (FIELD, 128), 1)

    def slope_of(which, goal_part, start):
        printed = jax.nn.sigmoid(6.0 * (part[which] + part_in[which] - 1.0))
        slope = 12.0 * (printed - goal_part) * printed * (1.0 - printed)
        line = start - RADIUS + tile * BAND
        slope = jnp.where((line >= 0) & (line < tiles * BAND), slope, 0.0)
        return jnp.concatenate([slope, slope], 1)

    swap_near.wait()
    slope = slope_of(0, goal_t[:, :128], lane)
    for k in range(BOTH):
        begun[k] = left_mul(back_c[...], slope * near[k])
    swap_far.wait()
    slope = slope_of(1, goal_far, 128 + lax.rem(lane, 64))
    for k in range(BOTH // 2):
        ended[k] = left_mul(back_c[...], slope * far[k])
    acc = [None, None]
    for k in range(BOTH):
        own = ended[k // 2, :, 128 * (k % 2) : 128 * (k % 2) + 128]
        low_rows = [jnp.where(first_half, own, 0.0), jnp.where(first_half, pltpu.roll(own, 64, 1), 0.0)]
        for c in range(2):
            head_rows = begun[k, :, 128 * c : 128 * c + 128]
            even, odd = head_rows + low_rows[c], head_rows - low_rows[c]
            streams[0, k, FX * c : FX * (c + 1), :] = spread(jnp.concatenate([even[:FX], even[FX:]], 1))
            streams[1, k, FX * c : FX * (c + 1), :] = spread(jnp.concatenate([odd[:FX], odd[FX:]], 1))
    for k in range(BOTH):
        for odd in range(2):
            wave = dot(streams[odd, k], rows_c[odd])
            for c in range(2):
                rows = slice(FX * c, FX * (c + 1))
                sr = spec[k, FX * c : FX * (c + 1), 256 * odd : 256 * odd + 128]
                si = spec[k, FX * c : FX * (c + 1), 256 * odd + 128 : 256 * odd + 256]
                gr, gi = wave[rows, :128], wave[rows, 128:]
                real, imag = sr * gr - si * gi, sr * gi + si * gr
                if acc[odd] is None:
                    acc[odd] = (real, imag)
                else:
                    acc[odd] = (acc[odd][0] + real, acc[odd][1] + imag)

    sign = 1.0 - 2.0 * lax.rem(lax.broadcasted_iota(jnp.int32, (FX, 128), 1), 2).astype(F32)
    even = jnp.concatenate([acc[0][0] * sign, acc[0][1] * sign], 1)
    odd = jnp.concatenate([-acc[1][1] * sign, acc[1][0] * sign], 1)
    back = right_mul(even, rows_t_c[0]) + right_mul(odd, rows_t_c[1])
    back = jnp.concatenate([back[:, :128], back[:, 128:]], 0)
    grad[...] = left_mul(last_c[...], back, dot)
    swap_2 = send(6, grad.at[pl.ds(64, 64)], grad_in, mate)
    swap_2.start()

    own = ext[64 : 64 + BAND, :]
    own = jnp.transpose(jnp.where(half == 0, own[:, :128], own[:, 128:]))
    own = jax.nn.sigmoid(3.0 * jnp.where(core == 0, own[:64], own[64:]))
    factor = 3.0 * own * (1.0 - own)
    swap_2.wait()
    result[...] = (grad[0:64, :] + grad_in[...]) * factor
    taps_over.wait_send()
    for copy in (mask_down, goal_down):
        pl.when(has_after)(copy.wait_send)
    for copy in (mask_up, goal_up):
        pl.when(has_before)(copy.wait_send)


def body(consts, mask_logit, target, kern_real, kern_imag, kern_weight):
    any_spec = pl.BlockSpec(memory_space=pltpu.HBM)
    vm = pltpu.VMEM
    scratch = [
        vm((NY, COLS), F32),
        vm((FROWS, COLS), jnp.int32),
        vm((OWN, TAPS, TAPS), F32),
        vm((OWN, TAPS, TAPS), F32),
        pltpu.SMEM((OWN,), F32),
        vm((2 * NX, 3 * 128), BF16),
        vm((NX, 128), F32),
        vm((2, 768, 256), BF16),
        vm((2, 768, 256), BF16),
        vm((NX, 3 * COLS), BF16),
        vm((FIELD, 3 * NX), BF16),
        vm((FIELD, COLS), BF16),
        vm((NX, 3 * FIELD), BF16),
        vm((128, 3 * NX), BF16),
        vm((2 * PACK, 128), F32),
        vm((BOTH, 2 * FX, 512), F32),
        vm((2, BOTH, 2 * FX, 768), BF16),
        vm((BOTH, 3 * NX, 256), BF16),
        vm((BOTH, FIELD, 256), F32),
        vm((BOTH // 2, FIELD, 256), F32),
        vm((BOTH, 2 * FX, 128), F32),
        vm((BOTH, 2 * FX, 256), F32),
        vm((BOTH // 2, 2 * FX, 256), F32),
        vm((2, FIELD, 128), F32),
        vm((2, FIELD, 128), F32),
        vm((128, BAND), F32),
        vm((64, BAND), F32),
        pltpu.SemaphoreType.DMA((14,)),
        pltpu.SemaphoreType.DMA((8,)),
        pltpu.SemaphoreType.DMA((8,)),
        pltpu.SemaphoreType.REGULAR,
    ]
    total = pl.pallas_call(
        kernel,
        out_shape=pltpu.VMEM((64, BAND), F32),
        in_specs=[any_spec] * (5 + len(NAMES)),
        out_specs=pl.BlockSpec(memory_space=pltpu.VMEM),
        scratch_shapes=scratch,
        compiler_params=pltpu.CompilerParams(
            collective_id=0, has_side_effects=True, vmem_limit_bytes=48 * 2**20
        ),
    )(*[pltpu.with_memory_space_constraint(v, pltpu.HBM) for v in (mask_logit, target, kern_real, kern_imag, kern_weight, *consts)])
    return total.T


def solution(mesh):
    made = tables()
    consts = [made[name] for name in NAMES]
    in_specs = (
        P("tile", None),
        P("tile", None),
        P("kern", None, None),
        P("kern", None, None),
        P("kern"),
    )
    mapped = jax.shard_map(
        lambda *args: body([jnp.asarray(c) for c in consts], *args),
        mesh=mesh, in_specs=in_specs, out_specs=P("tile", "kern"), check_vma=False,
    )
    return mapped
```

```python
import functools
import math

import jax
import jax.numpy as jnp
import ml_dtypes
import numpy as np
from jax import lax
from jax.experimental import pallas as pl
from jax.experimental.pallas import tpu as pltpu
from jax.sharding import PartitionSpec as P

F32 = jnp.float32
BF16 = jnp.bfloat16
MESH = pl.DeviceIdType.MESH

BAND = 128
COLS = 256
TAPS = 65
RADIUS = 32
OWN = 3
BOTH = 2 * OWN
NX = 224
FX = NX // 2
NY = 128
RUN = 16
PACK = 72 * OWN + 8
FIELD = 160
FROWS = 192


def triple(table, axis, order):
    high = table.astype(ml_dtypes.bfloat16)
    low = (table - high.astype(np.float64)).astype(ml_dtypes.bfloat16)
    return np.concatenate([(high, low)[i] for i in order], axis)


LEFT = (0, 1, 0)
RIGHT = (0, 0, 1)


def tables():
    theta = 2.0 * np.pi * (np.arange(FX) + 0.5) / NX

    def wave(offsets):
        angle = theta[:, None] * offsets[None, :]
        return np.concatenate([np.cos(angle), -np.sin(angle)], 0)

    scale = 2.0 / (NX * NY)
    into, back_in, out, last, pick = [], [], [], [], []
    for half in range(2):
        local = np.arange(COLS) - 64 * half
        full = wave(local) * ((local >= 0) & (local < 192))[None, :]
        into.append(triple(full, 1, LEFT))
        part = full[:, 96 * half : 96 * half + FIELD]
        back_in.append(triple(part, 1, LEFT))
        out.append(triple(scale * part.T, 1, LEFT))
        for core in range(2):
            cols = np.concatenate([64 * (2 * half + c) + np.arange(64) for c in (core, 1 - core)])
            last.append(triple(2.0 * scale * full[:, cols].T, 1, LEFT))
        pick.append((np.arange(COLS)[None, :] == np.arange(FIELD)[:, None] + 96 * half))
    taps = wave(np.arange(64) - RADIUS)
    zero = np.zeros_like(taps)
    taps = np.concatenate([np.concatenate([taps, zero], 1), np.concatenate([zero, taps], 1)], 0)
    edge = np.broadcast_to(wave(np.array([RADIUS])), (NX, 128))
    angle = 2.0 * np.pi * np.arange(NY)[:, None] * np.arange(NY)[None, :] / NY
    c, s = np.cos(angle), np.sin(angle)
    rows = np.concatenate([np.concatenate([c, -s], 1), np.concatenate([s, c], 1)], 0)
    return dict(
        rows=triple(rows, 0, RIGHT),
        rows_t=triple(rows.T, 0, RIGHT),
        into=np.stack(into),
        taps=triple(taps, 1, LEFT),
        edge=edge.astype(np.float32),
        out=np.stack(out),
        back_in=np.stack(back_in),
        last=np.stack(last),
        pick=np.stack(pick).astype(ml_dtypes.bfloat16),
    )


NAMES = ("taps", "edge", "rows", "rows_t", "into", "out", "pick", "back_in", "last")


def split(value):
    high = value.astype(BF16)
    return high, (value - high.astype(F32)).astype(BF16)


def dot(left, right):
    return jnp.dot(left, right, preferred_element_type=F32)


def dot_t(left, right):
    return lax.dot_general(left, right, (((1,), (1,)), ((), ())), preferred_element_type=F32)


def spread(value):
    high, low = split(value)
    return jnp.concatenate([high, low, high], 1)


def right_mul(value, table):
    return dot(spread(value), table)


def heap(value, axis=0):
    high, low = split(value)
    return jnp.concatenate([high, high, low], axis)


def left_mul(table, value, mul=dot):
    return mul(table, heap(value, 1 if mul is dot_t else 0))


def kernel(
    logit, target, kern_real, kern_imag, weight, taps_h, edge_h, rows_h, rows_t_h, into_h, out_h, pick_h, back_h, last_h,
    result,
    ext, goal, kr, ki, w, taps_c, edge_c, rows_c, rows_t_c, into_c, out_c, pick_c, back_c, last_c,
    packed, spec, columns, middle, lower, held, streams, waves, near, far, packs, begun, ended, part, part_in, grad, grad_in,
    local_sem, send_sem, recv_sem, relay,
):
    tile, kern = lax.axis_index("tile"), lax.axis_index("kern")
    tiles = lax.axis_size("tile")
    half, core = kern // 2, lax.rem(kern, 2)
    before = {"tile": lax.rem(tile + tiles - 1, tiles)}
    after = {"tile": lax.rem(tile + 1, tiles)}
    mate = {"kern": 2 * half + (1 - core)}
    across = {"kern": 2 * (1 - half) + core}
    beyond = {"tile": lax.rem(tile + tiles - 1, tiles), "kern": 2 * (1 - half) + core}
    onward = {"tile": lax.rem(tile + 1, tiles), "kern": 2 * (1 - half) + core}

    place = lax.rem(tile, RUN)
    head, tail = place == 0, place == RUN - 1
    eve = place == RUN - 2
    turn_before = head & (tile > 0)
    turn_after = tail & (tile < tiles - 1)

    barrier = pltpu.get_barrier_semaphore()

    def greet(device):
        pl.semaphore_signal(barrier, inc=1, device_id=device, device_id_type=MESH)

    inner = jnp.logical_not(tail)

    @pl.when(inner)
    def _():
        greet(across)
        greet(mate)

    pl.when(inner & jnp.logical_not(eve))(lambda: greet(after))
    pl.when(inner & jnp.logical_not(head))(lambda: greet(before))

    pairs = (
        (kern_real, kr),
        (kern_imag, ki),
        (weight, w),
        (taps_h, taps_c),
        (edge_h, edge_c),
        (rows_h, rows_c),
        (rows_t_h, rows_t_c),
        (logit, ext.at[pl.ds(64, BAND)]),
        (into_h.at[half], into_c),
        (out_h.at[half], out_c),
        (target, goal.at[pl.ds(RADIUS, BAND)]),
        (pick_h.at[half], pick_c),
        (back_h.at[half], back_c),
        (last_h.at[kern], last_c),
    )
    def send(index, src, dst, device, arrival=None):
        arrival = index if arrival is None else arrival
        return pltpu.make_async_remote_copy(
            src_ref=src, dst_ref=dst, send_sem=send_sem.at[index], recv_sem=recv_sem.at[arrival],
            device_id=device, device_id_type=MESH,
        )

    mask_down = send(0, logit.at[pl.ds(64, 64)], ext.at[pl.ds(0, 64)], after)
    mask_up = send(1, logit.at[pl.ds(0, 64)], ext.at[pl.ds(192, 64)], before)
    taps_over = send(2, packed.at[pl.ds(0, PACK)], packed.at[pl.ds(PACK, PACK)], across)
    taps_on = send(8, packed.at[pl.ds(0, PACK)], packed.at[pl.ds(PACK, PACK)], onward, 2)
    goal_down = send(3, target.at[pl.ds(96, RADIUS)], goal.at[pl.ds(0, RADIUS)], after)
    goal_up = send(4, target.at[pl.ds(0, RADIUS)], goal.at[pl.ds(160, RADIUS)], before)
    has_before, has_after = tile > 0, tile < tiles - 1

    @pl.when(turn_after)
    def _():
        pl.semaphore_wait(barrier, 1)
        mask_down.start()
        goal_down.start()
        greet(after)

    @pl.when(tail)
    def _():
        greet(before)
        greet(beyond)


    loads = [pltpu.make_async_copy(src, dst, local_sem.at[i]) for i, (src, dst) in enumerate(pairs)]
    for load in loads:
        load.start()

    for load in loads[:3]:
        load.wait()
    eye = lax.broadcasted_iota(jnp.int32, (TAPS, 128), 0) == lax.broadcasted_iota(jnp.int32, (TAPS, 128), 1)
    ends = []
    for k in range(OWN):
        factor = jnp.sqrt(jnp.full((TAPS, TAPS), w[k], F32))
        real, imag = kr[k] * factor, ki[k] * factor
        packed[72 * k + 64 : 72 * k + 72, :] = jnp.zeros((8, 128), F32)
        packed[72 * k : 72 * k + TAPS, :] = jnp.concatenate([real[:, 0:64], imag[:, 0:64]], axis=1)
        for grid in (real, imag):
            column = jnp.broadcast_to(grid[:, 64:65], (TAPS, 128))
            ends.append(jnp.sum(jnp.where(eye, column, 0.0), axis=0, keepdims=True))
    row_id = lax.broadcasted_iota(jnp.int32, (8, 128), 0)
    end_rows = jnp.zeros((8, 128), F32)
    for i, end in enumerate(ends):
        end_rows = jnp.where(row_id == i, jnp.broadcast_to(end, (8, 128)), end_rows)
    packed[72 * OWN : 72 * OWN + 8, :] = end_rows

    @pl.when(inner)
    def _():
        pl.semaphore_wait(barrier, 3 + jnp.where(head, 0, 1) + jnp.where(eve, 1, 0))
        pl.when(turn_before)(lambda: greet(before))
        pl.when(jnp.logical_not(head))(mask_up.start)
        taps_over.start()
        pl.when(eve)(taps_on.start)
        mask_down.start()
        goal_down.start()
        pl.when(jnp.logical_not(head))(goal_up.start)

    @pl.when(eve)
    def _():
        for device in (across, mate):
            pl.semaphore_signal(relay, inc=1, device_id=device, device_id_type=MESH)
        pl.semaphore_wait(relay, 2)
        greet(after)

    def mask_of(start, count):
        row = lax.broadcasted_iota(jnp.int32, (count, COLS), 0) + (start - 64) + tile * BAND
        inside = (row >= 0) & (row < tiles * BAND)
        return jnp.where(inside, jax.nn.sigmoid(3.0 * ext[start : start + count, :]), 0.0)

    first_half = lax.broadcasted_iota(jnp.int32, (1, 128), 1) < 64

    def halves(left, right):
        return jnp.where(first_half, left, pltpu.roll(right, 64, 1))

    def square(field):
        return field[:, :128] * field[:, :128] + field[:, 128:] * field[:, 128:]

    def beside(value):
        return jnp.concatenate([value[:FX], value[FX:]], 1)

    def above(value):
        return jnp.concatenate([value[:, :128], value[:, 128:]], 0)

    def rows_in(value):
        return right_mul(beside(value), rows_c[...])

    def times_mask(which, mask_spec, group):
        mr, mi = mask_spec[:, :128], mask_spec[:, 128:]
        for k in group:
            for c in range(2):
                sr, si = spec[k, FX * c : FX * (c + 1), :128], spec[k, FX * c : FX * (c + 1), 128:]
                streams[which, k, FX * c : FX * (c + 1), :] = spread(
                    jnp.concatenate([sr * mr + si * mi, sr * mi - si * mr], 1)
                )

    def gather(which):
        real, imag = None, None
        for k in range(BOTH):
            wave = dot(streams[which, k], rows_c[...])
            for c in range(2):
                sr, si = spec[k, FX * c : FX * (c + 1), :128], spec[k, FX * c : FX * (c + 1), 128:]
                gr, gi = wave[FX * c : FX * (c + 1), :128], wave[FX * c : FX * (c + 1), 128:]
                own_real, own_imag = sr * gr - si * gi, sr * gi + si * gr
                real = own_real if real is None else real + own_real
                imag = own_imag if imag is None else imag + own_imag
        return above(right_mul(jnp.concatenate([real, imag], 1), rows_t_c[...]))

    lane = lax.broadcasted_iota(jnp.int32, (FIELD, 128), 1)

    def slope_of(which, goal_part, line):
        printed = jax.nn.sigmoid(6.0 * (part[which] + part_in[which] - 1.0))
        slope = 12.0 * (printed - goal_part) * printed * (1.0 - printed)
        line = line - RADIUS + tile * BAND
        slope = jnp.where((line >= 0) & (line < tiles * BAND), slope, 0.0)
        return jnp.concatenate([slope, slope], 1)

    def spectrum(group):
        base = group * PACK
        ends = packed[base + 72 * OWN : base + PACK, :]
        edge = edge_c[...]
        for k in range(OWN):
            taps = jnp.concatenate([packed[base + 72 * k : base + 72 * k + 72, :], jnp.zeros((56, 128), F32)], 0)
            half_way = left_mul(taps_c[...], taps, dot_t)
            for c in range(2):
                row = ends[2 * k + c : 2 * k + c + 1, :]
                own = half_way[NX * c : NX * (c + 1)] + edge * row
                streams[0, k, FX * c : FX * (c + 1), :] = spread(jnp.concatenate([own[:FX], own[FX:]], 1))
        for k in range(OWN):
            spec[group * OWN + k] = dot(streams[0, k], rows_c[...])

    for load in loads[3:6]:
        load.wait()
    spectrum(0)

    @pl.when(tail)
    def _():
        pl.semaphore_wait(barrier, 1)
        mask_up.start()
        goal_up.start()

    own_taps, other_taps = range(OWN), range(OWN, BOTH)
    for load in loads[6:10]:
        load.wait()
    mask = jnp.concatenate([mask_of(128, 64), mask_of(64, 64)], 0)
    columns[...] = left_mul(into_c[...], mask, dot_t)
    middle[...] = rows_in(columns[...])

    def block_1(group):
        times_mask(0, middle[...], group)
        for k in group:
            held[k] = dot(streams[0, k], rows_t_c[...])

    def block_2(group):
        times_mask(1, lower[...], group)
        for k in group:
            block = dot(streams[1, k], rows_t_c[...])
            for c in range(2):
                rows = slice(FX * c, FX * (c + 1))
                real = jnp.where(first_half, block[rows, :128], held[k, rows, :128])
                imag = jnp.where(first_half, block[rows, 128:], held[k, rows, 128:])
                waves[k, :, 128 * c : 128 * c + 128] = heap(jnp.concatenate([real, imag], 0))

    def begin_block_2():
        pl.when(has_after)(mask_up.wait_recv)
        mask = jnp.concatenate([jnp.zeros((64, COLS), F32), mask_of(192, 64)], 0)
        lower[...] = rows_in(jnp.where(first_half, columns[...], left_mul(into_c[...], mask, dot_t)))
        block_2(own_taps)

    def block_0():
        pl.when(has_before)(mask_down.wait_recv)
        mask = jnp.concatenate([mask_of(0, 64), jnp.zeros((64, COLS), F32)], 0)
        upper = rows_in(jnp.where(first_half, left_mul(into_c[...], mask, dot_t), columns[...]))
        times_mask(0, upper, range(BOTH))
        for k in range(BOTH):
            block = dot(streams[0, k], rows_t_c[...])
            packs[k] = halves(above(block[:FX]), above(block[FX:]))
        total = None
        for k in range(BOTH // 2):
            field = left_mul(out_c[...], jnp.concatenate([packs[2 * k], packs[2 * k + 1]], 1))
            far[k] = field
            total = square(field) if total is None else total + square(field)
        part[1] = total + pltpu.roll(total, 64, 1)
        swap_far.start()

    swap_near = send(5, part.at[0], part_in.at[0], mate)
    swap_far = send(7, part.at[1], part_in.at[1], mate)

    block_1(own_taps)
    pl.when(inner)(begin_block_2)
    taps_over.wait_recv()
    spectrum(1)
    block_1(other_taps)
    pl.when(tail)(begin_block_2)
    block_2(other_taps)
    total = None
    for k in range(BOTH):
        field = dot(out_c[...], waves[k])
        near[k] = field
        total = square(field) if total is None else total + square(field)
    part[0] = total
    swap_near.start()
    pl.when(jnp.logical_not(turn_before))(block_0)

    pl.when(has_after)(goal_up.wait_recv)
    for load in loads[10:]:
        load.wait()
    goal_near = dot_t(pick_c[...], goal[64:192, :].astype(F32).astype(BF16))
    goal_near = pltpu.roll(goal_near, 64, 1)

    swap_near.wait()
    slope = slope_of(0, goal_near, jnp.where(lane < 64, lane + 128, lane))
    for k in range(BOTH):
        begun[k] = left_mul(back_c[...], slope * near[k])
    for k in range(BOTH):
        for c in range(2):
            streams[1, k, FX * c : FX * (c + 1), :] = spread(beside(begun[k, :, 128 * c : 128 * c + 128]))
    grad_tail = gather(1)

    @pl.when(turn_before)
    def _():
        pl.semaphore_wait(barrier, 1)
        mask_up.start()
        goal_up.start()
        block_0()

    pl.when(has_before)(goal_down.wait_recv)
    goal_rows = goal[0:64, :].astype(F32).astype(BF16)
    goal_far = dot_t(pick_c[...], jnp.concatenate([goal_rows, goal_rows], 0))

    swap_far.wait()
    slope = slope_of(1, goal_far, lax.rem(lane, 64))
    for k in range(BOTH // 2):
        ended[k] = left_mul(back_c[...], slope * far[k])
    for k in range(BOTH):
        own = ended[k // 2, :, 128 * (k % 2) : 128 * (k % 2) + 128]
        for c in range(2):
            source = own if c == 0 else pltpu.roll(own, 64, 1)
            source = jnp.where(first_half, source, begun[k, :, 128 * c : 128 * c + 128])
            streams[0, k, FX * c : FX * (c + 1), :] = spread(beside(source))
    back = pltpu.roll(jnp.where(first_half, grad_tail, gather(0)), 64, 1)
    grad[...] = left_mul(last_c[...], back)
    swap_2 = send(6, grad.at[pl.ds(64, 64)], grad_in, mate)
    swap_2.start()

    own = ext[64 : 64 + BAND, :]
    own = jnp.transpose(jnp.where(half == 0, own[:, :128], own[:, 128:]))
    own = jax.nn.sigmoid(3.0 * jnp.where(core == 0, own[:64], own[64:]))
    factor = 3.0 * own * (1.0 - own)
    swap_2.wait()
    result[...] = (grad[0:64, :] + grad_in[...]) * factor
    pl.when(inner)(taps_over.wait_send)
    pl.when(eve)(taps_on.wait_send)
    for copy in (mask_down, goal_down):
        pl.when(has_after)(copy.wait_send)
    for copy in (mask_up, goal_up):
        pl.when(has_before)(copy.wait_send)


def body(consts, mask_logit, target, kern_real, kern_imag, kern_weight):
    any_spec = pl.BlockSpec(memory_space=pltpu.HBM)
    vm = pltpu.VMEM
    scratch = [
        vm((256, COLS), F32),
        vm((FROWS, COLS), jnp.int32),
        vm((OWN, TAPS, TAPS), F32),
        vm((OWN, TAPS, TAPS), F32),
        pltpu.SMEM((OWN,), F32),
        vm((2 * NX, 3 * 128), BF16),
        vm((NX, 128), F32),
        vm((768, 256), BF16),
        vm((768, 256), BF16),
        vm((NX, 3 * COLS), BF16),
        vm((FIELD, 3 * NX), BF16),
        vm((FIELD, COLS), BF16),
        vm((NX, 3 * FIELD), BF16),
        vm((128, 3 * NX), BF16),
        vm((2 * PACK, 128), F32),
        vm((BOTH, 2 * FX, 256), F32),
        vm((NX, 128), F32),
        vm((FX, 256), F32),
        vm((FX, 256), F32),
        vm((BOTH, 2 * FX, 256), F32),
        vm((2, BOTH, 2 * FX, 768), BF16),
        vm((BOTH, 3 * NX, 256), BF16),
        vm((BOTH, FIELD, 256), F32),
        vm((BOTH // 2, FIELD, 256), F32),
        vm((BOTH, 2 * FX, 128), F32),
        vm((BOTH, 2 * FX, 256), F32),
        vm((BOTH // 2, 2 * FX, 256), F32),
        vm((2, FIELD, 128), F32),
        vm((2, FIELD, 128), F32),
        vm((128, BAND), F32),
        vm((64, BAND), F32),
        pltpu.SemaphoreType.DMA((14,)),
        pltpu.SemaphoreType.DMA((9,)),
        pltpu.SemaphoreType.DMA((9,)),
        pltpu.SemaphoreType.REGULAR,
    ]
    total = pl.pallas_call(
        kernel,
        out_shape=pltpu.VMEM((64, BAND), F32),
        in_specs=[any_spec] * (5 + len(NAMES)),
        out_specs=pl.BlockSpec(memory_space=pltpu.VMEM),
        scratch_shapes=scratch,
        compiler_params=pltpu.CompilerParams(
            collective_id=0, has_side_effects=True, vmem_limit_bytes=48 * 2**20
        ),
    )(*[pltpu.with_memory_space_constraint(v, pltpu.HBM) for v in (mask_logit, target, kern_real, kern_imag, kern_weight, *consts)])
    return total.T


def solution(mesh):
    made = tables()
    consts = [made[name] for name in NAMES]
    in_specs = (
        P("tile", None),
        P("tile", None),
        P("kern", None, None),
        P("kern", None, None),
        P("kern"),
    )
    mapped = jax.shard_map(
        lambda *args: body([jnp.asarray(c) for c in consts], *args),
        mesh=mesh, in_specs=in_specs, out_specs=P("tile", "kern"), check_vma=False,
    )
    return mapped
```

```python
import functools
import math

import jax
import jax.numpy as jnp
import ml_dtypes
import numpy as np
from jax import lax
from jax.experimental import pallas as pl
from jax.experimental.pallas import tpu as pltpu
from jax.sharding import PartitionSpec as P

F32 = jnp.float32
BF16 = jnp.bfloat16
MESH = pl.DeviceIdType.MESH

BAND = 128
COLS = 256
TAPS = 65
RADIUS = 32
OWN = 3
BOTH = 2 * OWN
NX = 224
FX = NX // 2
NY = 128
RUN = 16
PACK = 72 * OWN + 8
FIELD = 160
FROWS = 192


def triple(table, axis, order):
    high = table.astype(ml_dtypes.bfloat16)
    low = (table - high.astype(np.float64)).astype(ml_dtypes.bfloat16)
    return np.concatenate([(high, low)[i] for i in order], axis)


LEFT = (0, 1, 0)
RIGHT = (0, 0, 1)


def tables():
    theta = 2.0 * np.pi * (np.arange(FX) + 0.5) / NX

    def wave(offsets):
        angle = theta[:, None] * offsets[None, :]
        return np.concatenate([np.cos(angle), -np.sin(angle)], 0)

    scale = 2.0 / (NX * NY)
    into, back_in, out, last, pick = [], [], [], [], []
    for half in range(2):
        local = np.arange(COLS) - 64 * half
        full = wave(local) * ((local >= 0) & (local < 192))[None, :]
        into.append(triple(full, 1, LEFT))
        part = full[:, 96 * half : 96 * half + FIELD]
        back_in.append(triple(part, 1, LEFT))
        out.append(triple(scale * part.T, 1, LEFT))
        for core in range(2):
            cols = np.concatenate([64 * (2 * half + c) + np.arange(64) for c in (core, 1 - core)])
            last.append(triple(2.0 * scale * full[:, cols].T, 1, LEFT))
        pick.append((np.arange(COLS)[None, :] == np.arange(FIELD)[:, None] + 96 * half))
    taps = wave(np.arange(64) - RADIUS)
    zero = np.zeros_like(taps)
    taps = np.concatenate([np.concatenate([taps, zero], 1), np.concatenate([zero, taps], 1)], 0)
    edge = np.broadcast_to(wave(np.array([RADIUS])), (NX, 128))
    angle = 2.0 * np.pi * np.arange(NY)[:, None] * np.arange(NY)[None, :] / NY
    c, s = np.cos(angle), np.sin(angle)
    rows = np.concatenate([np.concatenate([c, -s], 1), np.concatenate([s, c], 1)], 0)
    return dict(
        rows=triple(rows, 0, RIGHT),
        rows_t=triple(rows.T, 0, RIGHT),
        into=np.stack(into),
        taps=triple(taps, 1, LEFT),
        edge=edge.astype(np.float32),
        out=np.stack(out),
        back_in=np.stack(back_in),
        last=np.stack(last),
        pick=np.stack(pick).astype(ml_dtypes.bfloat16),
    )


NAMES = ("taps", "edge", "rows", "rows_t", "into", "out", "pick", "back_in", "last")


def split(value):
    high = value.astype(BF16)
    return high, (value - high.astype(F32)).astype(BF16)


def dot(left, right):
    return jnp.dot(left, right, preferred_element_type=F32)


def dot_t(left, right):
    return lax.dot_general(left, right, (((1,), (1,)), ((), ())), preferred_element_type=F32)


def spread(value):
    high, low = split(value)
    return jnp.concatenate([high, low, high], 1)


def right_mul(value, table):
    return dot(spread(value), table)


def heap(value, axis=0):
    high, low = split(value)
    return jnp.concatenate([high, high, low], axis)


def left_mul(table, value, mul=dot):
    return mul(table, heap(value, 1 if mul is dot_t else 0))


def kernel(
    logit, target, kern_real, kern_imag, weight, taps_h, edge_h, rows_h, rows_t_h, into_h, out_h, pick_h, back_h, last_h,
    result,
    ext, goal, kr, ki, w, taps_c, edge_c, rows_c, rows_t_c, into_c, out_c, pick_c, back_c, last_c,
    packed, spare, spec, columns, middle, lower, held, streams, waves, near, far, packs, begun, ended, part, part_in, grad, grad_in,
    local_sem, send_sem, recv_sem, relay,
):
    tile, kern = lax.axis_index("tile"), lax.axis_index("kern")
    tiles = lax.axis_size("tile")
    half, core = kern // 2, lax.rem(kern, 2)
    before = {"tile": lax.rem(tile + tiles - 1, tiles)}
    after = {"tile": lax.rem(tile + 1, tiles)}
    mate = {"kern": 2 * half + (1 - core)}
    across = {"kern": 2 * (1 - half) + core}
    beyond = {"tile": lax.rem(tile + tiles - 1, tiles), "kern": 2 * (1 - half) + core}
    onward = {"tile": lax.rem(tile + 1, tiles), "kern": 2 * (1 - half) + core}

    place = lax.rem(tile, RUN)
    head, tail = place == 0, place == RUN - 1
    eve = place == RUN - 2
    turn_before = head & (tile > 0)
    turn_after = tail & (tile < tiles - 1)

    barrier = pltpu.get_barrier_semaphore()

    def greet(device):
        pl.semaphore_signal(barrier, inc=1, device_id=device, device_id_type=MESH)

    inner = jnp.logical_not(tail)

    corner = tile == 0
    served, server, giver = corner & (kern == 0), corner & (kern == 1), corner & (kern == 2)
    beside_served = (tile == 1) & (kern == 0)
    gives_up = jnp.logical_not(head | beside_served)

    @pl.when(inner)
    def _():
        pl.when(jnp.logical_not(served))(lambda: greet(across))
        pl.when(server)(lambda: greet({"kern": 2}))
        greet(mate)

    pl.when(inner & jnp.logical_not(eve | served))(lambda: greet(after))
    pl.when(inner & jnp.logical_not(head))(lambda: greet(before))

    pairs = (
        (kern_real, kr),
        (kern_imag, ki),
        (weight, w),
        (taps_h, taps_c),
        (edge_h, edge_c),
        (rows_h, rows_c),
        (rows_t_h, rows_t_c),
        (logit, ext.at[pl.ds(64, BAND)]),
        (into_h.at[half], into_c),
        (out_h.at[half], out_c),
        (target, goal.at[pl.ds(RADIUS, BAND)]),
        (pick_h.at[half], pick_c),
        (back_h.at[half], back_c),
        (last_h.at[kern], last_c),
    )
    def send(index, src, dst, device, arrival=None):
        arrival = index if arrival is None else arrival
        return pltpu.make_async_remote_copy(
            src_ref=src, dst_ref=dst, send_sem=send_sem.at[index], recv_sem=recv_sem.at[arrival],
            device_id=device, device_id_type=MESH,
        )

    mask_down = send(0, logit.at[pl.ds(64, 64)], ext.at[pl.ds(0, 64)], after)
    mask_up = send(1, logit.at[pl.ds(0, 64)], ext.at[pl.ds(192, 64)], before)
    taps_over = send(2, packed.at[pl.ds(0, PACK)], packed.at[pl.ds(PACK, PACK)], across)
    taps_on = send(8, packed.at[pl.ds(0, PACK)], packed.at[pl.ds(PACK, PACK)], onward, 2)
    taps_by = send(9, packed.at[pl.ds(0, PACK)], spare, {"kern": 1}, 8)
    mask_by = send(11, ext.at[pl.ds(192, 64)], ext.at[pl.ds(192, 64)], mate, 1)
    goal_by = send(12, goal.at[pl.ds(160, RADIUS)], goal.at[pl.ds(160, RADIUS)], mate, 4)
    taps_last = send(10, spare, packed.at[pl.ds(PACK, PACK)], mate, 2)
    goal_down = send(3, target.at[pl.ds(96, RADIUS)], goal.at[pl.ds(0, RADIUS)], after)
    goal_up = send(4, target.at[pl.ds(0, RADIUS)], goal.at[pl.ds(160, RADIUS)], before)
    has_before, has_after = tile > 0, tile < tiles - 1

    @pl.when(turn_after)
    def _():
        pl.semaphore_wait(barrier, 1)
        mask_down.start()
        goal_down.start()
        greet(after)

    @pl.when(tail)
    def _():
        greet(before)
        greet(beyond)


    loads = [pltpu.make_async_copy(src, dst, local_sem.at[i]) for i, (src, dst) in enumerate(pairs)]
    for load in loads:
        load.start()

    for load in loads[:3]:
        load.wait()
    eye = lax.broadcasted_iota(jnp.int32, (TAPS, 128), 0) == lax.broadcasted_iota(jnp.int32, (TAPS, 128), 1)
    ends = []
    for k in range(OWN):
        factor = jnp.sqrt(jnp.full((TAPS, TAPS), w[k], F32))
        real, imag = kr[k] * factor, ki[k] * factor
        packed[72 * k + 64 : 72 * k + 72, :] = jnp.zeros((8, 128), F32)
        packed[72 * k : 72 * k + TAPS, :] = jnp.concatenate([real[:, 0:64], imag[:, 0:64]], axis=1)
        for grid in (real, imag):
            column = jnp.broadcast_to(grid[:, 64:65], (TAPS, 128))
            ends.append(jnp.sum(jnp.where(eye, column, 0.0), axis=0, keepdims=True))
    row_id = lax.broadcasted_iota(jnp.int32, (8, 128), 0)
    end_rows = jnp.zeros((8, 128), F32)
    for i, end in enumerate(ends):
        end_rows = jnp.where(row_id == i, jnp.broadcast_to(end, (8, 128)), end_rows)
    packed[72 * OWN : 72 * OWN + 8, :] = end_rows

    @pl.when(inner)
    def _():
        pl.semaphore_wait(barrier, 3 + jnp.where(gives_up, 1, 0) + jnp.where(eve, 1, 0))
        pl.when(turn_before)(lambda: greet(before))
        pl.when(gives_up)(mask_up.start)
        pl.when(jnp.logical_not(giver))(taps_over.start)
        pl.when(giver)(taps_by.start)
        pl.when(eve)(taps_on.start)
        mask_down.start()
        goal_down.start()
        pl.when(gives_up)(goal_up.start)

    @pl.when(eve)
    def _():
        for device in (across, mate):
            pl.semaphore_signal(relay, inc=1, device_id=device, device_id_type=MESH)
        pl.semaphore_wait(relay, 2)
        greet(after)

    def mask_of(start, count):
        row = lax.broadcasted_iota(jnp.int32, (count, COLS), 0) + (start - 64) + tile * BAND
        inside = (row >= 0) & (row < tiles * BAND)
        return jnp.where(inside, jax.nn.sigmoid(3.0 * ext[start : start + count, :]), 0.0)

    first_half = lax.broadcasted_iota(jnp.int32, (1, 128), 1) < 64

    def halves(left, right):
        return jnp.where(first_half, left, pltpu.roll(right, 64, 1))

    def square(field):
        return field[:, :128] * field[:, :128] + field[:, 128:] * field[:, 128:]

    def beside(value):
        return jnp.concatenate([value[:FX], value[FX:]], 1)

    def above(value):
        return jnp.concatenate([value[:, :128], value[:, 128:]], 0)

    def rows_in(value):
        return right_mul(beside(value), rows_c[...])

    def times_mask(which, mask_spec, group):
        mr, mi = mask_spec[:, :128], mask_spec[:, 128:]
        for k in group:
            for c in range(2):
                sr, si = spec[k, FX * c : FX * (c + 1), :128], spec[k, FX * c : FX * (c + 1), 128:]
                streams[which, k, FX * c : FX * (c + 1), :] = spread(
                    jnp.concatenate([sr * mr + si * mi, sr * mi - si * mr], 1)
                )

    def gather(which):
        real, imag = None, None
        for k in range(BOTH):
            wave = dot(streams[which, k], rows_c[...])
            for c in range(2):
                sr, si = spec[k, FX * c : FX * (c + 1), :128], spec[k, FX * c : FX * (c + 1), 128:]
                gr, gi = wave[FX * c : FX * (c + 1), :128], wave[FX * c : FX * (c + 1), 128:]
                own_real, own_imag = sr * gr - si * gi, sr * gi + si * gr
                real = own_real if real is None else real + own_real
                imag = own_imag if imag is None else imag + own_imag
        return above(right_mul(jnp.concatenate([real, imag], 1), rows_t_c[...]))

    lane = lax.broadcasted_iota(jnp.int32, (FIELD, 128), 1)

    def slope_of(which, goal_part, line):
        printed = jax.nn.sigmoid(6.0 * (part[which] + part_in[which] - 1.0))
        slope = 12.0 * (printed - goal_part) * printed * (1.0 - printed)
        line = line - RADIUS + tile * BAND
        slope = jnp.where((line >= 0) & (line < tiles * BAND), slope, 0.0)
        return jnp.concatenate([slope, slope], 1)

    def spectrum(group):
        base = group * PACK
        ends = packed[base + 72 * OWN : base + PACK, :]
        edge = edge_c[...]
        for k in range(OWN):
            taps = jnp.concatenate([packed[base + 72 * k : base + 72 * k + 72, :], jnp.zeros((56, 128), F32)], 0)
            half_way = left_mul(taps_c[...], taps, dot_t)
            for c in range(2):
                row = ends[2 * k + c : 2 * k + c + 1, :]
                own = half_way[NX * c : NX * (c + 1)] + edge * row
                streams[0, k, FX * c : FX * (c + 1), :] = spread(jnp.concatenate([own[:FX], own[FX:]], 1))
        for k in range(OWN):
            spec[group * OWN + k] = dot(streams[0, k], rows_c[...])

    @pl.when(server)
    def _():
        mask_up.wait_recv()
        mask_by.start()
        goal_up.wait_recv()
        goal_by.start()

    for load in loads[3:6]:
        load.wait()
    spectrum(0)

    @pl.when(server)
    def _():
        taps_by.wait_recv()
        taps_last.start()

    @pl.when(tail)
    def _():
        pl.semaphore_wait(barrier, 1)
        mask_up.start()
        goal_up.start()

    own_taps, other_taps = range(OWN), range(OWN, BOTH)
    for load in loads[6:10]:
        load.wait()
    mask = jnp.concatenate([mask_of(128, 64), mask_of(64, 64)], 0)
    columns[...] = left_mul(into_c[...], mask, dot_t)
    middle[...] = rows_in(columns[...])

    def block_1(group):
        times_mask(0, middle[...], group)
        for k in group:
            held[k] = dot(streams[0, k], rows_t_c[...])

    def block_2(group):
        times_mask(1, lower[...], group)
        for k in group:
            block = dot(streams[1, k], rows_t_c[...])
            for c in range(2):
                rows = slice(FX * c, FX * (c + 1))
                real = jnp.where(first_half, block[rows, :128], held[k, rows, :128])
                imag = jnp.where(first_half, block[rows, 128:], held[k, rows, 128:])
                waves[k, :, 128 * c : 128 * c + 128] = heap(jnp.concatenate([real, imag], 0))

    def begin_block_2():
        pl.when(has_after & jnp.logical_not(server))(mask_up.wait_recv)
        mask = jnp.concatenate([jnp.zeros((64, COLS), F32), mask_of(192, 64)], 0)
        lower[...] = rows_in(jnp.where(first_half, columns[...], left_mul(into_c[...], mask, dot_t)))
        block_2(own_taps)

    def block_0():
        pl.when(has_before)(mask_down.wait_recv)
        mask = jnp.concatenate([mask_of(0, 64), jnp.zeros((64, COLS), F32)], 0)
        upper = rows_in(jnp.where(first_half, left_mul(into_c[...], mask, dot_t), columns[...]))
        times_mask(0, upper, range(BOTH))
        for k in range(BOTH):
            block = dot(streams[0, k], rows_t_c[...])
            packs[k] = halves(above(block[:FX]), above(block[FX:]))
        total = None
        for k in range(BOTH // 2):
            field = left_mul(out_c[...], jnp.concatenate([packs[2 * k], packs[2 * k + 1]], 1))
            far[k] = field
            total = square(field) if total is None else total + square(field)
        part[1] = total + pltpu.roll(total, 64, 1)
        swap_far.start()

    swap_near = send(5, part.at[0], part_in.at[0], mate)
    swap_far = send(7, part.at[1], part_in.at[1], mate)

    block_1(own_taps)
    pl.when(inner)(begin_block_2)
    taps_over.wait_recv()
    spectrum(1)
    block_1(other_taps)
    pl.when(tail)(begin_block_2)
    block_2(other_taps)
    total = None
    for k in range(BOTH):
        field = dot(out_c[...], waves[k])
        near[k] = field
        total = square(field) if total is None else total + square(field)
    part[0] = total
    swap_near.start()
    pl.when(jnp.logical_not(turn_before))(block_0)

    pl.when(has_after & jnp.logical_not(server))(goal_up.wait_recv)
    for load in loads[10:]:
        load.wait()
    goal_near = dot_t(pick_c[...], goal[64:192, :].astype(F32).astype(BF16))
    goal_near = pltpu.roll(goal_near, 64, 1)

    swap_near.wait()
    slope = slope_of(0, goal_near, jnp.where(lane < 64, lane + 128, lane))
    for k in range(BOTH):
        begun[k] = left_mul(back_c[...], slope * near[k])
    for k in range(BOTH):
        for c in range(2):
            streams[1, k, FX * c : FX * (c + 1), :] = spread(beside(begun[k, :, 128 * c : 128 * c + 128]))
    grad_tail = gather(1)

    @pl.when(turn_before)
    def _():
        pl.semaphore_wait(barrier, 1)
        mask_up.start()
        goal_up.start()
        block_0()

    pl.when(has_before)(goal_down.wait_recv)
    goal_rows = goal[0:64, :].astype(F32).astype(BF16)
    goal_far = dot_t(pick_c[...], jnp.concatenate([goal_rows, goal_rows], 0))

    swap_far.wait()
    slope = slope_of(1, goal_far, lax.rem(lane, 64))
    for k in range(BOTH // 2):
        ended[k] = left_mul(back_c[...], slope * far[k])
    for k in range(BOTH):
        own = ended[k // 2, :, 128 * (k % 2) : 128 * (k % 2) + 128]
        for c in range(2):
            source = own if c == 0 else pltpu.roll(own, 64, 1)
            source = jnp.where(first_half, source, begun[k, :, 128 * c : 128 * c + 128])
            streams[0, k, FX * c : FX * (c + 1), :] = spread(beside(source))
    back = pltpu.roll(jnp.where(first_half, grad_tail, gather(0)), 64, 1)
    grad[...] = left_mul(last_c[...], back)
    swap_2 = send(6, grad.at[pl.ds(64, 64)], grad_in, mate)
    swap_2.start()

    own = ext[64 : 64 + BAND, :]
    own = jnp.transpose(jnp.where(half == 0, own[:, :128], own[:, 128:]))
    own = jax.nn.sigmoid(3.0 * jnp.where(core == 0, own[:64], own[64:]))
    factor = 3.0 * own * (1.0 - own)
    swap_2.wait()
    result[...] = (grad[0:64, :] + grad_in[...]) * factor
    pl.when(inner & jnp.logical_not(giver))(taps_over.wait_send)
    pl.when(giver)(taps_by.wait_send)
    pl.when(server)(taps_last.wait_send)
    pl.when(eve)(taps_on.wait_send)
    for copy in (mask_down, goal_down):
        pl.when(has_after)(copy.wait_send)
    for copy in (mask_up, goal_up):
        pl.when(has_before & jnp.logical_not(beside_served))(copy.wait_send)
    for copy in (mask_by, goal_by):
        pl.when(server)(copy.wait_send)


def body(consts, mask_logit, target, kern_real, kern_imag, kern_weight):
    any_spec = pl.BlockSpec(memory_space=pltpu.HBM)
    vm = pltpu.VMEM
    scratch = [
        vm((256, COLS), F32),
        vm((FROWS, COLS), jnp.int32),
        vm((OWN, TAPS, TAPS), F32),
        vm((OWN, TAPS, TAPS), F32),
        pltpu.SMEM((OWN,), F32),
        vm((2 * NX, 3 * 128), BF16),
        vm((NX, 128), F32),
        vm((768, 256), BF16),
        vm((768, 256), BF16),
        vm((NX, 3 * COLS), BF16),
        vm((FIELD, 3 * NX), BF16),
        vm((FIELD, COLS), BF16),
        vm((NX, 3 * FIELD), BF16),
        vm((128, 3 * NX), BF16),
        vm((2 * PACK, 128), F32),
        vm((PACK, 128), F32),
        vm((BOTH, 2 * FX, 256), F32),
        vm((NX, 128), F32),
        vm((FX, 256), F32),
        vm((FX, 256), F32),
        vm((BOTH, 2 * FX, 256), F32),
        vm((2, BOTH, 2 * FX, 768), BF16),
        vm((BOTH, 3 * NX, 256), BF16),
        vm((BOTH, FIELD, 256), F32),
        vm((BOTH // 2, FIELD, 256), F32),
        vm((BOTH, 2 * FX, 128), F32),
        vm((BOTH, 2 * FX, 256), F32),
        vm((BOTH // 2, 2 * FX, 256), F32),
        vm((2, FIELD, 128), F32),
        vm((2, FIELD, 128), F32),
        vm((128, BAND), F32),
        vm((64, BAND), F32),
        pltpu.SemaphoreType.DMA((14,)),
        pltpu.SemaphoreType.DMA((13,)),
        pltpu.SemaphoreType.DMA((13,)),
        pltpu.SemaphoreType.REGULAR,
    ]
    total = pl.pallas_call(
        kernel,
        out_shape=pltpu.VMEM((64, BAND), F32),
        in_specs=[any_spec] * (5 + len(NAMES)),
        out_specs=pl.BlockSpec(memory_space=pltpu.VMEM),
        scratch_shapes=scratch,
        compiler_params=pltpu.CompilerParams(
            collective_id=0, has_side_effects=True, vmem_limit_bytes=48 * 2**20
        ),
    )(*[pltpu.with_memory_space_constraint(v, pltpu.HBM) for v in (mask_logit, target, kern_real, kern_imag, kern_weight, *consts)])
    return total.T


def solution(mesh):
    made = tables()
    consts = [made[name] for name in NAMES]
    in_specs = (
        P("tile", None),
        P("tile", None),
        P("kern", None, None),
        P("kern", None, None),
        P("kern"),
    )
    mapped = jax.shard_map(
        lambda *args: body([jnp.asarray(c) for c in consts], *args),
        mesh=mesh, in_specs=in_specs, out_specs=P("tile", "kern"), check_vma=False,
    )
    return mapped
```

```python
import functools
import math

import jax
import jax.numpy as jnp
import ml_dtypes
import numpy as np
from jax import lax
from jax.experimental import pallas as pl
from jax.experimental.pallas import tpu as pltpu
from jax.sharding import PartitionSpec as P

F32 = jnp.float32
BF16 = jnp.bfloat16
MESH = pl.DeviceIdType.MESH

BAND = 128
COLS = 256
TAPS = 65
RADIUS = 32
OWN = 3
BOTH = 2 * OWN
NX = 224
FX = NX // 2
NY = 128
RUN = 16
PACK = 72 * OWN + 8
FIELD = 160
FROWS = 192


def triple(table, axis, order):
    high = table.astype(ml_dtypes.bfloat16)
    low = (table - high.astype(np.float64)).astype(ml_dtypes.bfloat16)
    return np.concatenate([(high, low)[i] for i in order], axis)


LEFT = (0, 1, 0)
RIGHT = (0, 0, 1)


def tables():
    theta = 2.0 * np.pi * (np.arange(FX) + 0.5) / NX

    def wave(offsets):
        angle = theta[:, None] * offsets[None, :]
        return np.concatenate([np.cos(angle), -np.sin(angle)], 0)

    scale = 2.0 / (NX * NY)
    into, back_in, out, last, pick = [], [], [], [], []
    for half in range(2):
        local = np.arange(COLS) - 64 * half
        full = wave(local) * ((local >= 0) & (local < 192))[None, :]
        into.append(triple(full, 1, LEFT))
        part = full[:, 96 * half : 96 * half + FIELD]
        back_in.append(triple(part, 1, LEFT))
        out.append(triple(scale * part.T, 1, LEFT))
        for core in range(2):
            cols = np.concatenate([64 * (2 * half + c) + np.arange(64) for c in (core, 1 - core)])
            last.append(triple(2.0 * scale * full[:, cols].T, 1, LEFT))
        pick.append((np.arange(COLS)[None, :] == np.arange(FIELD)[:, None] + 96 * half))
    taps = wave(np.arange(64) - RADIUS)
    zero = np.zeros_like(taps)
    taps = np.concatenate([np.concatenate([taps, zero], 1), np.concatenate([zero, taps], 1)], 0)
    edge = np.broadcast_to(wave(np.array([RADIUS])), (NX, 128))
    angle = 2.0 * np.pi * np.arange(NY)[:, None] * np.arange(NY)[None, :] / NY
    c, s = np.cos(angle), np.sin(angle)
    rows = np.concatenate([np.concatenate([c, -s], 1), np.concatenate([s, c], 1)], 0)
    return dict(
        rows=triple(rows, 0, RIGHT),
        rows_t=triple(rows.T, 0, RIGHT),
        into=np.stack(into),
        taps=triple(taps, 1, LEFT),
        edge=edge.astype(np.float32),
        out=np.stack(out),
        back_in=np.stack(back_in),
        last=np.stack(last),
        pick=np.stack(pick).astype(ml_dtypes.bfloat16),
    )


NAMES = ("taps", "edge", "rows", "rows_t", "into", "out", "pick", "back_in", "last")


def split(value):
    high = value.astype(BF16)
    return high, (value - high.astype(F32)).astype(BF16)


def dot(left, right):
    return jnp.dot(left, right, preferred_element_type=F32)


def dot_t(left, right):
    return lax.dot_general(left, right, (((1,), (1,)), ((), ())), preferred_element_type=F32)


def spread(value):
    high, low = split(value)
    return jnp.concatenate([high, low, high], 1)


def right_mul(value, table):
    return dot(spread(value), table)


def heap(value, axis=0):
    high, low = split(value)
    return jnp.concatenate([high, high, low], axis)


def left_mul(table, value, mul=dot):
    return mul(table, heap(value, 1 if mul is dot_t else 0))


def kernel(
    logit, target, kern_real, kern_imag, weight, taps_h, edge_h, rows_h, rows_t_h, into_h, out_h, pick_h, back_h, last_h,
    result,
    ext, goal, kr, ki, w, taps_c, edge_c, rows_c, rows_t_c, into_c, out_c, pick_c, back_c, last_c,
    packed, spare, spec, columns, middle, lower, held, streams, waves, near, far, packs, begun, ended, part, part_in, grad, grad_in,
    local_sem, send_sem, recv_sem, relay,
):
    tile, kern = lax.axis_index("tile"), lax.axis_index("kern")
    tiles = lax.axis_size("tile")
    half, core = kern // 2, lax.rem(kern, 2)
    before = {"tile": lax.rem(tile + tiles - 1, tiles)}
    after = {"tile": lax.rem(tile + 1, tiles)}
    mate = {"kern": 2 * half + (1 - core)}
    across = {"kern": 2 * (1 - half) + core}
    beyond = {"tile": lax.rem(tile + tiles - 1, tiles), "kern": 2 * (1 - half) + core}
    onward = {"tile": lax.rem(tile + 1, tiles), "kern": 2 * (1 - half) + core}

    place = lax.rem(tile, RUN)
    head, tail = place == 0, place == RUN - 1
    eve = place == RUN - 2
    turn_before = head & (tile > 0)
    turn_after = tail & (tile < tiles - 1)

    barrier = pltpu.get_barrier_semaphore()

    def greet(device):
        pl.semaphore_signal(barrier, inc=1, device_id=device, device_id_type=MESH)

    inner = jnp.logical_not(tail)

    corner = tile == 0
    served, server, giver = corner & (kern == 0), corner & (kern == 1), corner & (kern == 2)
    beside_served = (tile == 1) & (kern == 0)
    gives_up = jnp.logical_not(head | beside_served)

    @pl.when(inner)
    def _():
        pl.when(jnp.logical_not(served))(lambda: greet(across))
        pl.when(server)(lambda: greet({"kern": 2}))
        greet(mate)

    pl.when(inner & jnp.logical_not(eve | served))(lambda: greet(after))
    pl.when(inner & jnp.logical_not(head))(lambda: greet(before))

    pairs = (
        (kern_real, kr),
        (kern_imag, ki),
        (weight, w),
        (taps_h, taps_c),
        (edge_h, edge_c),
        (rows_h, rows_c),
        (rows_t_h, rows_t_c),
        (logit, ext.at[pl.ds(64, BAND)]),
        (into_h.at[half], into_c),
        (out_h.at[half], out_c),
        (target, goal.at[pl.ds(RADIUS, BAND)]),
        (pick_h.at[half], pick_c),
        (back_h.at[half], back_c),
        (last_h.at[kern], last_c),
    )
    def send(index, src, dst, device, arrival=None):
        arrival = index if arrival is None else arrival
        return pltpu.make_async_remote_copy(
            src_ref=src, dst_ref=dst, send_sem=send_sem.at[index], recv_sem=recv_sem.at[arrival],
            device_id=device, device_id_type=MESH,
        )

    mask_down = send(0, logit.at[pl.ds(64, 64)], ext.at[pl.ds(0, 64)], after)
    mask_up = send(1, logit.at[pl.ds(0, 64)], ext.at[pl.ds(192, 64)], before)
    taps_over = send(2, packed.at[pl.ds(0, PACK)], packed.at[pl.ds(PACK, PACK)], across)
    taps_on = send(8, packed.at[pl.ds(0, PACK)], packed.at[pl.ds(PACK, PACK)], onward, 2)
    taps_by = send(9, packed.at[pl.ds(0, PACK)], spare, {"kern": 1}, 8)
    mask_by = send(11, ext.at[pl.ds(192, 64)], ext.at[pl.ds(192, 64)], mate, 1)
    goal_by = send(12, goal.at[pl.ds(160, RADIUS)], goal.at[pl.ds(160, RADIUS)], mate, 4)
    taps_last = send(10, spare, packed.at[pl.ds(PACK, PACK)], mate, 2)
    goal_down = send(3, target.at[pl.ds(96, RADIUS)], goal.at[pl.ds(0, RADIUS)], after)
    goal_up = send(4, target.at[pl.ds(0, RADIUS)], goal.at[pl.ds(160, RADIUS)], before)
    has_before, has_after = tile > 0, tile < tiles - 1

    @pl.when(turn_after)
    def _():
        pl.semaphore_wait(barrier, 1)
        mask_down.start()
        goal_down.start()
        greet(after)

    @pl.when(tail)
    def _():
        greet(before)
        greet(beyond)


    loads = [pltpu.make_async_copy(src, dst, local_sem.at[i]) for i, (src, dst) in enumerate(pairs)]
    for load in loads:
        load.start()

    for load in loads[:3]:
        load.wait()
    eye = lax.broadcasted_iota(jnp.int32, (TAPS, 128), 0) == lax.broadcasted_iota(jnp.int32, (TAPS, 128), 1)
    ends = []
    for k in range(OWN):
        factor = jnp.sqrt(jnp.full((TAPS, TAPS), w[k], F32))
        real, imag = kr[k] * factor, ki[k] * factor
        packed[72 * k + 64 : 72 * k + 72, :] = jnp.zeros((8, 128), F32)
        packed[72 * k : 72 * k + TAPS, :] = jnp.concatenate([real[:, 0:64], imag[:, 0:64]], axis=1)
        for grid in (real, imag):
            column = jnp.broadcast_to(grid[:, 64:65], (TAPS, 128))
            ends.append(jnp.sum(jnp.where(eye, column, 0.0), axis=0, keepdims=True))
    row_id = lax.broadcasted_iota(jnp.int32, (8, 128), 0)
    end_rows = jnp.zeros((8, 128), F32)
    for i, end in enumerate(ends):
        end_rows = jnp.where(row_id == i, jnp.broadcast_to(end, (8, 128)), end_rows)
    packed[72 * OWN : 72 * OWN + 8, :] = end_rows

    @pl.when(inner)
    def _():
        pl.semaphore_wait(barrier, 3 + jnp.where(gives_up, 1, 0) + jnp.where(eve, 1, 0))
        pl.when(turn_before)(lambda: greet(before))

        @pl.when(eve)
        def _():
            for device in (across, mate):
                pl.semaphore_signal(relay, inc=1, device_id=device, device_id_type=MESH)
            taps_on.start()

        pl.when(gives_up)(mask_up.start)
        pl.when(jnp.logical_not(giver))(taps_over.start)
        pl.when(giver)(taps_by.start)
        mask_down.start()
        goal_down.start()
        pl.when(gives_up)(goal_up.start)

    @pl.when(eve)
    def _():
        pl.semaphore_wait(relay, 2)
        greet(after)

    def mask_of(start, count):
        row = lax.broadcasted_iota(jnp.int32, (count, COLS), 0) + (start - 64) + tile * BAND
        inside = (row >= 0) & (row < tiles * BAND)
        return jnp.where(inside, jax.nn.sigmoid(3.0 * ext[start : start + count, :]), 0.0)

    first_half = lax.broadcasted_iota(jnp.int32, (1, 128), 1) < 64

    def halves(left, right):
        return jnp.where(first_half, left, pltpu.roll(right, 64, 1))

    def square(field):
        return field[:, :128] * field[:, :128] + field[:, 128:] * field[:, 128:]

    def beside(value):
        return jnp.concatenate([value[:FX], value[FX:]], 1)

    def above(value):
        return jnp.concatenate([value[:, :128], value[:, 128:]], 0)

    def rows_in(value):
        return right_mul(beside(value), rows_c[...])

    def times_mask(which, mask_spec, group):
        mr, mi = mask_spec[:, :128], mask_spec[:, 128:]
        for k in group:
            for c in range(2):
                sr, si = spec[k, FX * c : FX * (c + 1), :128], spec[k, FX * c : FX * (c + 1), 128:]
                streams[which, k, FX * c : FX * (c + 1), :] = spread(
                    jnp.concatenate([sr * mr + si * mi, sr * mi - si * mr], 1)
                )

    def gather(which):
        real, imag = None, None
        for k in range(BOTH):
            wave = dot(streams[which, k], rows_c[...])
            for c in range(2):
                sr, si = spec[k, FX * c : FX * (c + 1), :128], spec[k, FX * c : FX * (c + 1), 128:]
                gr, gi = wave[FX * c : FX * (c + 1), :128], wave[FX * c : FX * (c + 1), 128:]
                own_real, own_imag = sr * gr - si * gi, sr * gi + si * gr
                real = own_real if real is None else real + own_real
                imag = own_imag if imag is None else imag + own_imag
        return above(right_mul(jnp.concatenate([real, imag], 1), rows_t_c[...]))

    lane = lax.broadcasted_iota(jnp.int32, (FIELD, 128), 1)

    def slope_of(which, goal_part, line):
        printed = jax.nn.sigmoid(6.0 * (part[which] + part_in[which] - 1.0))
        slope = 12.0 * (printed - goal_part) * printed * (1.0 - printed)
        line = line - RADIUS + tile * BAND
        slope = jnp.where((line >= 0) & (line < tiles * BAND), slope, 0.0)
        return jnp.concatenate([slope, slope], 1)

    def spectrum(group):
        base = group * PACK
        ends = packed[base + 72 * OWN : base + PACK, :]
        edge = edge_c[...]
        gap = jnp.zeros((56, 128), F32)
        taps = [jnp.concatenate([packed[base + 72 * k : base + 72 * k + 72, :], gap], 0) for k in range(OWN)]
        pair = left_mul(taps_c[...], jnp.concatenate(taps[:2], 0), dot_t)
        half_ways = [pair[:, :128], pair[:, 128:], left_mul(taps_c[...], taps[2], dot_t)]
        for k in range(OWN):
            for c in range(2):
                row = ends[2 * k + c : 2 * k + c + 1, :]
                own = half_ways[k][NX * c : NX * (c + 1)] + edge * row
                streams[0, k, FX * c : FX * (c + 1), :] = spread(jnp.concatenate([own[:FX], own[FX:]], 1))
        for k in range(OWN):
            spec[group * OWN + k] = dot(streams[0, k], rows_c[...])

    @pl.when(server)
    def _():
        mask_up.wait_recv()
        mask_by.start()
        goal_up.wait_recv()
        goal_by.start()

    for load in loads[3:6]:
        load.wait()
    spectrum(0)

    @pl.when(server)
    def _():
        taps_by.wait_recv()
        taps_last.start()

    @pl.when(tail)
    def _():
        pl.semaphore_wait(barrier, 1)
        mask_up.start()
        goal_up.start()

    own_taps, other_taps = range(OWN), range(OWN, BOTH)
    for load in loads[6:10]:
        load.wait()
    mask = jnp.concatenate([mask_of(128, 64), mask_of(64, 64)], 0)
    columns[...] = left_mul(into_c[...], mask, dot_t)
    middle[...] = rows_in(columns[...])

    def block_1(group):
        times_mask(0, middle[...], group)
        for k in group:
            held[k] = dot(streams[0, k], rows_t_c[...])

    def block_2(group):
        times_mask(1, lower[...], group)
        for k in group:
            block = dot(streams[1, k], rows_t_c[...])
            for c in range(2):
                rows = slice(FX * c, FX * (c + 1))
                real = jnp.where(first_half, block[rows, :128], held[k, rows, :128])
                imag = jnp.where(first_half, block[rows, 128:], held[k, rows, 128:])
                waves[k, :, 128 * c : 128 * c + 128] = heap(jnp.concatenate([real, imag], 0))

    def begin_block_2():
        pl.when(has_after & jnp.logical_not(server))(mask_up.wait_recv)
        mask = jnp.concatenate([jnp.zeros((64, COLS), F32), mask_of(192, 64)], 0)
        lower[...] = rows_in(jnp.where(first_half, columns[...], left_mul(into_c[...], mask, dot_t)))
        block_2(own_taps)

    def block_0():
        pl.when(has_before)(mask_down.wait_recv)
        mask = jnp.concatenate([mask_of(0, 64), jnp.zeros((64, COLS), F32)], 0)
        upper = rows_in(jnp.where(first_half, left_mul(into_c[...], mask, dot_t), columns[...]))
        times_mask(0, upper, range(BOTH))
        for k in range(BOTH):
            block = dot(streams[0, k], rows_t_c[...])
            packs[k] = halves(above(block[:FX]), above(block[FX:]))
        total = None
        for k in range(BOTH // 2):
            field = left_mul(out_c[...], jnp.concatenate([packs[2 * k], packs[2 * k + 1]], 1))
            far[k] = field
            total = square(field) if total is None else total + square(field)
        part[1] = total + pltpu.roll(total, 64, 1)
        swap_far.start()

    swap_near = send(5, part.at[0], part_in.at[0], mate)
    swap_far = send(7, part.at[1], part_in.at[1], mate)

    block_1(own_taps)
    pl.when(inner)(begin_block_2)
    taps_over.wait_recv()
    spectrum(1)
    block_1(other_taps)
    pl.when(tail)(begin_block_2)
    block_2(other_taps)
    total = None
    for k in range(BOTH):
        field = dot(out_c[...], waves[k])
        near[k] = field
        total = square(field) if total is None else total + square(field)
    part[0] = total
    swap_near.start()
    pl.when(jnp.logical_not(turn_before))(block_0)

    pl.when(has_after & jnp.logical_not(server))(goal_up.wait_recv)
    for load in loads[10:]:
        load.wait()
    goal_near = dot_t(pick_c[...], goal[64:192, :].astype(F32).astype(BF16))
    goal_near = pltpu.roll(goal_near, 64, 1)


    @pl.when(turn_before)
    def _():
        pl.semaphore_wait(barrier, 1)
        mask_up.start()
        goal_up.start()

    swap_near.wait()
    slope = slope_of(0, goal_near, jnp.where(lane < 64, lane + 128, lane))
    for k in range(BOTH):
        begun[k] = left_mul(back_c[...], slope * near[k])
    for k in range(BOTH):
        for c in range(2):
            streams[1, k, FX * c : FX * (c + 1), :] = spread(beside(begun[k, :, 128 * c : 128 * c + 128]))
    grad_tail = gather(1)

    pl.when(turn_before)(block_0)

    pl.when(has_before)(goal_down.wait_recv)
    goal_rows = goal[0:64, :].astype(F32).astype(BF16)
    goal_far = dot_t(pick_c[...], jnp.concatenate([goal_rows, goal_rows], 0))

    swap_far.wait()
    slope = slope_of(1, goal_far, lax.rem(lane, 64))
    for k in range(BOTH // 2):
        ended[k] = left_mul(back_c[...], slope * far[k])
    for k in range(BOTH):
        own = ended[k // 2, :, 128 * (k % 2) : 128 * (k % 2) + 128]
        for c in range(2):
            source = own if c == 0 else pltpu.roll(own, 64, 1)
            source = jnp.where(first_half, source, begun[k, :, 128 * c : 128 * c + 128])
            streams[0, k, FX * c : FX * (c + 1), :] = spread(beside(source))
    back = pltpu.roll(jnp.where(first_half, grad_tail, gather(0)), 64, 1)
    grad[...] = left_mul(last_c[...], back)
    swap_2 = send(6, grad.at[pl.ds(64, 64)], grad_in, mate)
    swap_2.start()

    own = ext[64 : 64 + BAND, :]
    own = jnp.transpose(jnp.where(half == 0, own[:, :128], own[:, 128:]))
    own = jax.nn.sigmoid(3.0 * jnp.where(core == 0, own[:64], own[64:]))
    factor = 3.0 * own * (1.0 - own)
    swap_2.wait()
    result[...] = (grad[0:64, :] + grad_in[...]) * factor
    pl.when(inner & jnp.logical_not(giver))(taps_over.wait_send)
    pl.when(giver)(taps_by.wait_send)
    pl.when(server)(taps_last.wait_send)
    pl.when(eve)(taps_on.wait_send)
    for copy in (mask_down, goal_down):
        pl.when(has_after)(copy.wait_send)
    for copy in (mask_up, goal_up):
        pl.when(has_before & jnp.logical_not(beside_served))(copy.wait_send)
    for copy in (mask_by, goal_by):
        pl.when(server)(copy.wait_send)


def body(consts, mask_logit, target, kern_real, kern_imag, kern_weight):
    any_spec = pl.BlockSpec(memory_space=pltpu.HBM)
    vm = pltpu.VMEM
    scratch = [
        vm((256, COLS), F32),
        vm((FROWS, COLS), jnp.int32),
        vm((OWN, TAPS, TAPS), F32),
        vm((OWN, TAPS, TAPS), F32),
        pltpu.SMEM((OWN,), F32),
        vm((2 * NX, 3 * 128), BF16),
        vm((NX, 128), F32),
        vm((768, 256), BF16),
        vm((768, 256), BF16),
        vm((NX, 3 * COLS), BF16),
        vm((FIELD, 3 * NX), BF16),
        vm((FIELD, COLS), BF16),
        vm((NX, 3 * FIELD), BF16),
        vm((128, 3 * NX), BF16),
        vm((2 * PACK, 128), F32),
        vm((PACK, 128), F32),
        vm((BOTH, 2 * FX, 256), F32),
        vm((NX, 128), F32),
        vm((FX, 256), F32),
        vm((FX, 256), F32),
        vm((BOTH, 2 * FX, 256), F32),
        vm((2, BOTH, 2 * FX, 768), BF16),
        vm((BOTH, 3 * NX, 256), BF16),
        vm((BOTH, FIELD, 256), F32),
        vm((BOTH // 2, FIELD, 256), F32),
        vm((BOTH, 2 * FX, 128), F32),
        vm((BOTH, 2 * FX, 256), F32),
        vm((BOTH // 2, 2 * FX, 256), F32),
        vm((2, FIELD, 128), F32),
        vm((2, FIELD, 128), F32),
        vm((128, BAND), F32),
        vm((64, BAND), F32),
        pltpu.SemaphoreType.DMA((14,)),
        pltpu.SemaphoreType.DMA((13,)),
        pltpu.SemaphoreType.DMA((13,)),
        pltpu.SemaphoreType.REGULAR,
    ]
    total = pl.pallas_call(
        kernel,
        out_shape=pltpu.VMEM((64, BAND), F32),
        in_specs=[any_spec] * (5 + len(NAMES)),
        out_specs=pl.BlockSpec(memory_space=pltpu.VMEM),
        scratch_shapes=scratch,
        compiler_params=pltpu.CompilerParams(
            collective_id=0, has_side_effects=True, vmem_limit_bytes=48 * 2**20
        ),
    )(*[pltpu.with_memory_space_constraint(v, pltpu.HBM) for v in (mask_logit, target, kern_real, kern_imag, kern_weight, *consts)])
    return total.T


def solution(mesh):
    made = tables()
    consts = [made[name] for name in NAMES]
    in_specs = (
        P("tile", None),
        P("tile", None),
        P("kern", None, None),
        P("kern", None, None),
        P("kern"),
    )
    mapped = jax.shard_map(
        lambda *args: body([jnp.asarray(c) for c in consts], *args),
        mesh=mesh, in_specs=in_specs, out_specs=P("tile", "kern"), check_vma=False,
    )
    return mapped
```

```python
import functools
import math

import jax
import jax.numpy as jnp
import ml_dtypes
import numpy as np
from jax import lax
from jax.experimental import pallas as pl
from jax.experimental.pallas import tpu as pltpu
from jax.sharding import PartitionSpec as P

F32 = jnp.float32
BF16 = jnp.bfloat16
MESH = pl.DeviceIdType.MESH

BAND = 128
COLS = 256
TAPS = 65
RADIUS = 32
OWN = 3
BOTH = 2 * OWN
NX = 224
FX = NX // 2
NY = 128
RUN = 16
PACK = 72 * OWN + 8
FIELD = 160
FROWS = 192


def triple(table, axis, order):
    high = table.astype(ml_dtypes.bfloat16)
    low = (table - high.astype(np.float64)).astype(ml_dtypes.bfloat16)
    return np.concatenate([(high, low)[i] for i in order], axis)


LEFT = (0, 1, 0)
RIGHT = (0, 0, 1)


def tables():
    theta = 2.0 * np.pi * (np.arange(FX) + 0.5) / NX

    def wave(offsets):
        angle = theta[:, None] * offsets[None, :]
        return np.concatenate([np.cos(angle), -np.sin(angle)], 0)

    scale = 2.0 / (NX * NY)
    into, back_in, out, last, pick = [], [], [], [], []
    for half in range(2):
        local = np.arange(COLS) - 64 * half
        full = wave(local) * ((local >= 0) & (local < 192))[None, :]
        into.append(triple(full, 1, LEFT))
        part = full[:, 96 * half : 96 * half + FIELD]
        back_in.append(triple(part, 1, LEFT))
        out.append(triple(scale * part.T, 1, LEFT))
        for core in range(2):
            cols = np.concatenate([64 * (2 * half + c) + np.arange(64) for c in (core, 1 - core)])
            last.append(triple(2.0 * scale * full[:, cols].T, 1, LEFT))
        pick.append((np.arange(COLS)[None, :] == np.arange(FIELD)[:, None] + 96 * half))
    taps = wave(np.arange(64) - RADIUS)
    zero = np.zeros_like(taps)
    taps = np.concatenate([np.concatenate([taps, zero], 1), np.concatenate([zero, taps], 1)], 0)
    edge = np.broadcast_to(wave(np.array([RADIUS])), (NX, 128))
    angle = 2.0 * np.pi * np.arange(NY)[:, None] * np.arange(NY)[None, :] / NY
    c, s = np.cos(angle), np.sin(angle)
    rows = np.concatenate([np.concatenate([c, -s], 1), np.concatenate([s, c], 1)], 0)
    return dict(
        rows=triple(rows, 0, RIGHT),
        rows_t=triple(rows.T, 0, RIGHT),
        into=np.stack(into),
        taps=triple(taps, 1, LEFT),
        edge=edge.astype(np.float32),
        out=np.stack(out),
        back_in=np.stack(back_in),
        last=np.stack(last),
        pick=np.stack(pick).astype(ml_dtypes.bfloat16),
    )


NAMES = ("taps", "edge", "rows", "rows_t", "into", "out", "pick", "back_in", "last")


def split(value):
    high = value.astype(BF16)
    return high, (value - high.astype(F32)).astype(BF16)


def dot(left, right):
    return jnp.dot(left, right, preferred_element_type=F32)


def dot_t(left, right):
    return lax.dot_general(left, right, (((1,), (1,)), ((), ())), preferred_element_type=F32)


def spread(value):
    high, low = split(value)
    return jnp.concatenate([high, low, high], 1)


def right_mul(value, table):
    return dot(spread(value), table)


def heap(value, axis=0):
    high, low = split(value)
    return jnp.concatenate([high, high, low], axis)


def left_mul(table, value, mul=dot):
    return mul(table, heap(value, 1 if mul is dot_t else 0))


def kernel(
    logit, target, kern_real, kern_imag, weight, taps_h, edge_h, rows_h, rows_t_h, into_h, out_h, pick_h, back_h, last_h,
    result,
    ext, goal, kr, ki, w, taps_c, edge_c, rows_c, rows_t_c, into_c, out_c, pick_c, back_c, last_c,
    packed, spare, spec, columns, middle, lower, held, streams, waves, near, far, packs, begun, ended, part, part_in, grad, grad_in,
    local_sem, send_sem, recv_sem, relay,
):
    tile, kern = lax.axis_index("tile"), lax.axis_index("kern")
    tiles = lax.axis_size("tile")
    half, core = kern // 2, lax.rem(kern, 2)
    before = {"tile": lax.rem(tile + tiles - 1, tiles)}
    after = {"tile": lax.rem(tile + 1, tiles)}
    mate = {"kern": 2 * half + (1 - core)}
    across = {"kern": 2 * (1 - half) + core}
    beyond = {"tile": lax.rem(tile + tiles - 1, tiles), "kern": 2 * (1 - half) + core}
    onward = {"tile": lax.rem(tile + 1, tiles), "kern": 2 * (1 - half) + core}

    place = lax.rem(tile, RUN)
    head, tail = place == 0, place == RUN - 1
    eve = place == RUN - 2
    turn_before = head & (tile > 0)
    turn_after = tail & (tile < tiles - 1)

    barrier = pltpu.get_barrier_semaphore()

    def greet(device):
        pl.semaphore_signal(barrier, inc=1, device_id=device, device_id_type=MESH)

    inner = jnp.logical_not(tail)

    corner = tile == 0
    served, server, giver = corner & (kern == 0), corner & (kern == 1), corner & (kern == 2)
    beside_served = (tile == 1) & (kern == 0)
    gives_up = jnp.logical_not(head | beside_served)

    @pl.when(inner)
    def _():
        pl.when(jnp.logical_not(served))(lambda: greet(across))
        pl.when(server)(lambda: greet({"kern": 2}))
        greet(mate)

    pl.when(inner & jnp.logical_not(eve | served))(lambda: greet(after))
    pl.when(inner & jnp.logical_not(head))(lambda: greet(before))

    pairs = (
        (kern_real, kr),
        (kern_imag, ki),
        (weight, w),
        (taps_h, taps_c),
        (edge_h, edge_c),
        (rows_h, rows_c),
        (rows_t_h, rows_t_c),
        (logit, ext.at[pl.ds(64, BAND)]),
        (into_h.at[half], into_c),
        (out_h.at[half], out_c),
        (target, goal.at[pl.ds(RADIUS, BAND)]),
        (pick_h.at[half], pick_c),
        (back_h.at[half], back_c),
        (last_h.at[kern], last_c),
    )
    def send(index, src, dst, device, arrival=None):
        arrival = index if arrival is None else arrival
        return pltpu.make_async_remote_copy(
            src_ref=src, dst_ref=dst, send_sem=send_sem.at[index], recv_sem=recv_sem.at[arrival],
            device_id=device, device_id_type=MESH,
        )

    mask_down = send(0, logit.at[pl.ds(64, 64)], ext.at[pl.ds(0, 64)], after)
    mask_up = send(1, logit.at[pl.ds(0, 64)], ext.at[pl.ds(192, 64)], before)
    taps_over = send(2, packed.at[pl.ds(0, PACK)], packed.at[pl.ds(PACK, PACK)], across)
    taps_on = send(8, packed.at[pl.ds(0, PACK)], packed.at[pl.ds(PACK, PACK)], onward, 2)
    taps_by = send(9, packed.at[pl.ds(0, PACK)], spare, {"kern": 1}, 8)
    mask_by = send(11, ext.at[pl.ds(192, 64)], ext.at[pl.ds(192, 64)], mate, 1)
    goal_by = send(12, goal.at[pl.ds(160, RADIUS)], goal.at[pl.ds(160, RADIUS)], mate, 4)
    taps_last = send(10, spare, packed.at[pl.ds(PACK, PACK)], mate, 2)
    goal_down = send(3, target.at[pl.ds(96, RADIUS)], goal.at[pl.ds(0, RADIUS)], after)
    goal_up = send(4, target.at[pl.ds(0, RADIUS)], goal.at[pl.ds(160, RADIUS)], before)
    has_before, has_after = tile > 0, tile < tiles - 1

    @pl.when(turn_after)
    def _():
        pl.semaphore_wait(barrier, 1)
        mask_down.start()
        goal_down.start()
        greet(after)

    @pl.when(tail)
    def _():
        greet(before)
        greet(beyond)


    loads = [pltpu.make_async_copy(src, dst, local_sem.at[i]) for i, (src, dst) in enumerate(pairs)]
    for load in loads:
        load.start()

    for load in loads[:3]:
        load.wait()
    eye = lax.broadcasted_iota(jnp.int32, (TAPS, 128), 0) == lax.broadcasted_iota(jnp.int32, (TAPS, 128), 1)
    ends = []
    for k in range(OWN):
        factor = jnp.sqrt(jnp.full((TAPS, TAPS), w[k], F32))
        real, imag = kr[k] * factor, ki[k] * factor
        packed[72 * k + 64 : 72 * k + 72, :] = jnp.zeros((8, 128), F32)
        packed[72 * k : 72 * k + TAPS, :] = jnp.concatenate([real[:, 0:64], imag[:, 0:64]], axis=1)
        for grid in (real, imag):
            column = jnp.broadcast_to(grid[:, 64:65], (TAPS, 128))
            ends.append(jnp.sum(jnp.where(eye, column, 0.0), axis=0, keepdims=True))
    row_id = lax.broadcasted_iota(jnp.int32, (8, 128), 0)
    end_rows = jnp.zeros((8, 128), F32)
    for i, end in enumerate(ends):
        end_rows = jnp.where(row_id == i, jnp.broadcast_to(end, (8, 128)), end_rows)
    packed[72 * OWN : 72 * OWN + 8, :] = end_rows

    @pl.when(inner)
    def _():
        pl.semaphore_wait(barrier, 3 + jnp.where(gives_up, 1, 0) + jnp.where(eve, 1, 0))
        pl.when(turn_before)(lambda: greet(before))
        pl.when(gives_up)(mask_up.start)
        pl.when(jnp.logical_not(giver))(taps_over.start)
        pl.when(giver)(taps_by.start)
        pl.when(eve)(taps_on.start)
        mask_down.start()
        goal_down.start()
        pl.when(gives_up)(goal_up.start)

    @pl.when(eve)
    def _():
        for device in (across, mate):
            pl.semaphore_signal(relay, inc=1, device_id=device, device_id_type=MESH)
        pl.semaphore_wait(relay, 2)
        greet(after)

    def mask_of(start, count):
        row = lax.broadcasted_iota(jnp.int32, (count, COLS), 0) + (start - 64) + tile * BAND
        inside = (row >= 0) & (row < tiles * BAND)
        return jnp.where(inside, jax.nn.sigmoid(3.0 * ext[start : start + count, :]), 0.0)

    first_half = lax.broadcasted_iota(jnp.int32, (1, 128), 1) < 64

    def halves(left, right):
        return jnp.where(first_half, left, pltpu.roll(right, 64, 1))

    def square(field):
        return field[:, :128] * field[:, :128] + field[:, 128:] * field[:, 128:]

    def beside(value):
        return jnp.concatenate([value[:FX], value[FX:]], 1)

    def above(value):
        return jnp.concatenate([value[:, :128], value[:, 128:]], 0)

    def rows_in(value):
        return right_mul(beside(value), rows_c[...])

    def times_mask(which, mask_spec, group):
        mr, mi = mask_spec[:, :128], mask_spec[:, 128:]
        for k in group:
            for c in range(2):
                sr, si = spec[k, FX * c : FX * (c + 1), :128], spec[k, FX * c : FX * (c + 1), 128:]
                streams[which, k, FX * c : FX * (c + 1), :] = spread(
                    jnp.concatenate([sr * mr + si * mi, sr * mi - si * mr], 1)
                )

    def gather(which):
        real, imag = None, None
        for k in range(BOTH):
            wave = dot(streams[which, k], rows_c[...])
            for c in range(2):
                sr, si = spec[k, FX * c : FX * (c + 1), :128], spec[k, FX * c : FX * (c + 1), 128:]
                gr, gi = wave[FX * c : FX * (c + 1), :128], wave[FX * c : FX * (c + 1), 128:]
                own_real, own_imag = sr * gr - si * gi, sr * gi + si * gr
                real = own_real if real is None else real + own_real
                imag = own_imag if imag is None else imag + own_imag
        return above(right_mul(jnp.concatenate([real, imag], 1), rows_t_c[...]))

    lane = lax.broadcasted_iota(jnp.int32, (FIELD, 128), 1)

    def slope_of(which, goal_part, line):
        rows = goal_part.shape[0]
        printed = jax.nn.sigmoid(6.0 * (part[which, 0:rows, :] + part_in[which, 0:rows, :] - 1.0))
        slope = 12.0 * (printed - goal_part) * printed * (1.0 - printed)
        line = line - RADIUS + tile * BAND
        slope = jnp.where((line >= 0) & (line < tiles * BAND), slope, 0.0)
        return jnp.concatenate([slope, slope], 1)

    def spectrum(group):
        base = group * PACK
        ends = packed[base + 72 * OWN : base + PACK, :]
        edge = edge_c[...]
        for k in range(OWN):
            taps = jnp.concatenate([packed[base + 72 * k : base + 72 * k + 72, :], jnp.zeros((56, 128), F32)], 0)
            half_way = left_mul(taps_c[...], taps, dot_t)
            for c in range(2):
                row = ends[2 * k + c : 2 * k + c + 1, :]
                own = half_way[NX * c : NX * (c + 1)] + edge * row
                streams[0, k, FX * c : FX * (c + 1), :] = spread(jnp.concatenate([own[:FX], own[FX:]], 1))
        for k in range(OWN):
            spec[group * OWN + k] = dot(streams[0, k], rows_c[...])

    @pl.when(server)
    def _():
        mask_up.wait_recv()
        mask_by.start()
        goal_up.wait_recv()
        goal_by.start()

    for load in loads[3:6]:
        load.wait()
    spectrum(0)

    @pl.when(server)
    def _():
        taps_by.wait_recv()
        taps_last.start()

    @pl.when(tail)
    def _():
        pl.semaphore_wait(barrier, 1)
        mask_up.start()
        goal_up.start()

    own_taps, other_taps = range(OWN), range(OWN, BOTH)
    for load in loads[6:10]:
        load.wait()
    mask = jnp.concatenate([mask_of(128, 64), mask_of(64, 64)], 0)
    columns[...] = left_mul(into_c[...], mask, dot_t)
    middle[...] = rows_in(columns[...])

    def block_1(group):
        times_mask(0, middle[...], group)
        for k in group:
            held[k] = dot(streams[0, k], rows_t_c[...])

    def block_2(group):
        times_mask(1, lower[...], group)
        for k in group:
            block = dot(streams[1, k], rows_t_c[...])
            for c in range(2):
                rows = slice(FX * c, FX * (c + 1))
                real = jnp.where(first_half, block[rows, :128], held[k, rows, :128])
                imag = jnp.where(first_half, block[rows, 128:], held[k, rows, 128:])
                waves[k, :, 128 * c : 128 * c + 128] = heap(jnp.concatenate([real, imag], 0))

    def begin_block_2():
        pl.when(has_after & jnp.logical_not(server))(mask_up.wait_recv)
        mask = jnp.concatenate([jnp.zeros((64, COLS), F32), mask_of(192, 64)], 0)
        lower[...] = rows_in(jnp.where(first_half, columns[...], left_mul(into_c[...], mask, dot_t)))
        block_2(own_taps)

    def block_0():
        pl.when(has_before)(mask_down.wait_recv)
        mask = jnp.concatenate([mask_of(0, 64), jnp.zeros((64, COLS), F32)], 0)
        upper = rows_in(jnp.where(first_half, left_mul(into_c[...], mask, dot_t), columns[...]))
        times_mask(0, upper, range(BOTH))
        for k in range(BOTH):
            block = dot(streams[0, k], rows_t_c[...])
            packs[k] = halves(above(block[:FX]), above(block[FX:]))
        total = None
        for k in range(BOTH // 2):
            field = left_mul(out_c[...], jnp.concatenate([packs[2 * k], packs[2 * k + 1]], 1))
            far[k] = field
            total = square(field) if total is None else total + square(field)
        total = total + pltpu.roll(total, 64, 1)
        part[1, 0:80, :] = jnp.where(first_half, total[:80], total[80:])
        swap_far.start()

    swap_near = send(5, part.at[0], part_in.at[0], mate)
    swap_far = send(7, part.at[1, pl.ds(0, 80)], part_in.at[1, pl.ds(0, 80)], mate)

    block_1(own_taps)
    pl.when(inner)(begin_block_2)
    taps_over.wait_recv()
    spectrum(1)
    block_1(other_taps)
    pl.when(tail)(begin_block_2)
    block_2(other_taps)
    total = None
    for k in range(BOTH):
        field = dot(out_c[...], waves[k])
        near[k] = field
        total = square(field) if total is None else total + square(field)
    part[0] = total
    swap_near.start()
    pl.when(jnp.logical_not(turn_before))(block_0)

    pl.when(has_after & jnp.logical_not(server))(goal_up.wait_recv)
    for load in loads[10:]:
        load.wait()
    goal_near = dot_t(pick_c[...], goal[64:192, :].astype(F32).astype(BF16))
    goal_near = pltpu.roll(goal_near, 64, 1)

    swap_near.wait()
    slope = slope_of(0, goal_near, jnp.where(lane < 64, lane + 128, lane))
    for k in range(BOTH):
        begun[k] = left_mul(back_c[...], slope * near[k])
    for k in range(BOTH):
        for c in range(2):
            streams[1, k, FX * c : FX * (c + 1), :] = spread(beside(begun[k, :, 128 * c : 128 * c + 128]))
    grad_tail = gather(1)

    @pl.when(turn_before)
    def _():
        pl.semaphore_wait(barrier, 1)
        mask_up.start()
        goal_up.start()
        block_0()

    pl.when(has_before)(goal_down.wait_recv)
    goal_rows = goal[0:64, :].astype(F32).astype(BF16)
    goal_far = dot_t(pick_c[...], jnp.concatenate([goal_rows, goal_rows], 0))

    swap_far.wait()
    slope = slope_of(1, jnp.where(first_half, goal_far[:80], goal_far[80:]), lax.rem(lane[:80], 64))[:, :128]
    turned = pltpu.roll(slope, 64, 1)
    slope = jnp.concatenate([jnp.where(first_half, slope, turned), jnp.where(first_half, turned, slope)], 0)
    slope = jnp.concatenate([slope, slope], 1)
    for k in range(BOTH // 2):
        ended[k] = left_mul(back_c[...], slope * far[k])
    for k in range(BOTH):
        own = ended[k // 2, :, 128 * (k % 2) : 128 * (k % 2) + 128]
        for c in range(2):
            source = own if c == 0 else pltpu.roll(own, 64, 1)
            source = jnp.where(first_half, source, begun[k, :, 128 * c : 128 * c + 128])
            streams[0, k, FX * c : FX * (c + 1), :] = spread(beside(source))
    back = pltpu.roll(jnp.where(first_half, grad_tail, gather(0)), 64, 1)
    grad[...] = left_mul(last_c[...], back)
    swap_2 = send(6, grad.at[pl.ds(64, 64)], grad_in, mate)
    swap_2.start()

    own = ext[64 : 64 + BAND, :]
    own = jnp.transpose(jnp.where(half == 0, own[:, :128], own[:, 128:]))
    own = jax.nn.sigmoid(3.0 * jnp.where(core == 0, own[:64], own[64:]))
    factor = 3.0 * own * (1.0 - own)
    swap_2.wait()
    result[...] = (grad[0:64, :] + grad_in[...]) * factor
    pl.when(inner & jnp.logical_not(giver))(taps_over.wait_send)
    pl.when(giver)(taps_by.wait_send)
    pl.when(server)(taps_last.wait_send)
    pl.when(eve)(taps_on.wait_send)
    for copy in (mask_down, goal_down):
        pl.when(has_after)(copy.wait_send)
    for copy in (mask_up, goal_up):
        pl.when(has_before & jnp.logical_not(beside_served))(copy.wait_send)
    for copy in (mask_by, goal_by):
        pl.when(server)(copy.wait_send)


def body(consts, mask_logit, target, kern_real, kern_imag, kern_weight):
    any_spec = pl.BlockSpec(memory_space=pltpu.HBM)
    vm = pltpu.VMEM
    scratch = [
        vm((256, COLS), F32),
        vm((FROWS, COLS), jnp.int32),
        vm((OWN, TAPS, TAPS), F32),
        vm((OWN, TAPS, TAPS), F32),
        pltpu.SMEM((OWN,), F32),
        vm((2 * NX, 3 * 128), BF16),
        vm((NX, 128), F32),
        vm((768, 256), BF16),
        vm((768, 256), BF16),
        vm((NX, 3 * COLS), BF16),
        vm((FIELD, 3 * NX), BF16),
        vm((FIELD, COLS), BF16),
        vm((NX, 3 * FIELD), BF16),
        vm((128, 3 * NX), BF16),
        vm((2 * PACK, 128), F32),
        vm((PACK, 128), F32),
        vm((BOTH, 2 * FX, 256), F32),
        vm((NX, 128), F32),
        vm((FX, 256), F32),
        vm((FX, 256), F32),
        vm((BOTH, 2 * FX, 256), F32),
        vm((2, BOTH, 2 * FX, 768), BF16),
        vm((BOTH, 3 * NX, 256), BF16),
        vm((BOTH, FIELD, 256), F32),
        vm((BOTH // 2, FIELD, 256), F32),
        vm((BOTH, 2 * FX, 128), F32),
        vm((BOTH, 2 * FX, 256), F32),
        vm((BOTH // 2, 2 * FX, 256), F32),
        vm((2, FIELD, 128), F32),
        vm((2, FIELD, 128), F32),
        vm((128, BAND), F32),
        vm((64, BAND), F32),
        pltpu.SemaphoreType.DMA((14,)),
        pltpu.SemaphoreType.DMA((13,)),
        pltpu.SemaphoreType.DMA((13,)),
        pltpu.SemaphoreType.REGULAR,
    ]
    total = pl.pallas_call(
        kernel,
        out_shape=pltpu.VMEM((64, BAND), F32),
        in_specs=[any_spec] * (5 + len(NAMES)),
        out_specs=pl.BlockSpec(memory_space=pltpu.VMEM),
        scratch_shapes=scratch,
        compiler_params=pltpu.CompilerParams(
            collective_id=0, has_side_effects=True, vmem_limit_bytes=48 * 2**20
        ),
    )(*[pltpu.with_memory_space_constraint(v, pltpu.HBM) for v in (mask_logit, target, kern_real, kern_imag, kern_weight, *consts)])
    return total.T


def solution(mesh):
    made = tables()
    consts = [made[name] for name in NAMES]
    in_specs = (
        P("tile", None),
        P("tile", None),
        P("kern", None, None),
        P("kern", None, None),
        P("kern"),
    )
    mapped = jax.shard_map(
        lambda *args: body([jnp.asarray(c) for c in consts], *args),
        mesh=mesh, in_specs=in_specs, out_specs=P("tile", "kern"), check_vma=False,
    )
    return mapped
```
